32 devices in a mesh: bucket: 2 (over y), row: 4 (over x, core), col: 4 (over z).
Axes of the slice: x: 2, y: 2, z: 4, core: 2. Of those that a mesh axis runs over, the one named last changes fastest.
Arguments:
- left_docs: bfloat16 [2048, 4096], P(('bucket', 'row'), 'col'), parts along dimension 0, may hold values from -30 to 30
- right_docs: bfloat16 [1024, 4096], P(('bucket', 'col'), 'row'), parts along dimension 0, may hold values from -30 to 30
Outputs:
- similarity: float32 [2048, 512], P(('bucket', 'row'), 'col'), parts along dimension 0
The draws below stay inside these ranges and needn't reach their ends.
There are 2 independent parts, one for each index of `bucket`. The reference program is written for one: setup_inputs(seed, part) draws one part's arguments, and reference() takes and returns one part's arrays. A program takes and returns all parts, laid end to end along the dimension named above; each array names one. Nothing has to cross between parts.
All inputs are finite; a program needn't handle non-finite values.
Results may differ from the reference program's by a relative error of at most 0.0003.
Values may be sent and summed in bfloat16 or wider, within the bound.
No kernel may reach another device: no remote copies, remote signals or barrier semaphores. Data moves between devices by JAX's collectives and lax.ppermute only.
A program may use at most 64 MiB of HBM per device.

```python
import math
import jax
import jax.numpy as jnp
from jax import lax

LEFT_DOCS = 1024
RIGHT_DOCS = 512
FEAT = 4096


cluster_count = 8


def shared_parts(key):
    cluster_base = jax.random.truncated_normal(jax.random.fold_in(key, 101), -4.0, 4.0, (cluster_count, FEAT), jnp.float32)
    rising = 3.0 ** (jnp.arange(FEAT, dtype=jnp.float32) / FEAT)
    spread = jnp.exp(jax.random.uniform(jax.random.fold_in(key, 102), (FEAT,), jnp.float32) * math.log(10.0))
    return (cluster_base, rising * spread / 10.0)


def make_docs(key, count, jitter, mix_top):
    cluster_base, feature_scale = shared_parts(key)
    cluster_ids = jax.random.randint(jax.random.fold_in(key, 201), (count,), 0, cluster_count)
    mixing = jax.random.uniform(jax.random.fold_in(key, 202), (count, 1), jnp.float32, 0.3, mix_top)
    row_scale = jnp.exp(jax.random.uniform(jax.random.fold_in(key, 203), (count, 1), jnp.float32) * math.log(10.0))
    documents = jnp.take(cluster_base, cluster_ids, axis=0) * mixing + jitter
    return documents * feature_scale[None, :] * row_scale / 10.0


def draw_left_docs(key, part):
    folded = jax.random.fold_in(key, 1)
    jitter = jax.random.truncated_normal(folded, -4.0, 4.0, (LEFT_DOCS, FEAT), jnp.float32)
    documents = make_docs(key, LEFT_DOCS, jitter, 1.5)
    return documents.astype(jnp.bfloat16)


def draw_right_docs(key, part):
    folded = jax.random.fold_in(key, 2)
    inner = jax.random.fold_in(key, 7)
    jitter = jax.random.truncated_normal(folded, -4.0, 4.0, (RIGHT_DOCS, FEAT), jnp.float32)
    documents = make_docs(inner, RIGHT_DOCS, jitter, 1.5)
    return documents.astype(jnp.bfloat16)


def setup_inputs(seed: int = 0, part: int = 0) -> dict:
    splits = jax.random.split(jax.random.key(seed), 3)
    own_keys = jax.random.split(jax.random.fold_in(splits[2], part), 3)
    left_docs = draw_left_docs(jax.random.fold_in(jax.random.fold_in(splits[2], part), 71), part)
    right_docs = draw_right_docs(jax.random.fold_in(jax.random.fold_in(splits[2], part), 71), part)
    return {"left_docs": left_docs, "right_docs": right_docs}


def reference(left_docs, right_docs):
    left_wide = left_docs.astype(jnp.float32)
    right_wide = right_docs.astype(jnp.float32)
    gram_tile = lax.dot_general(left_wide, right_wide, (((1,), (1,)), ((), ())), precision=lax.Precision.HIGHEST, preferred_element_type=jnp.float32)
    left_power = lax.optimization_barrier(jnp.mean(left_wide * left_wide, axis=1))
    right_power = lax.optimization_barrier(jnp.mean(right_wide * right_wide, axis=1))
    left_scale = lax.rsqrt(left_power + 1e-06)
    right_scale = lax.rsqrt(right_power + 1e-06)
    return gram_tile / FEAT * left_scale[:, None] * right_scale[None, :]
```

```python
import jax
import jax.numpy as jnp
from jax import lax
from jax.sharding import PartitionSpec as P

epsilon = 1e-06


def contract(left_part, right_part):
    return lax.dot_general(
        left_part, right_part, (((1,), (1,)), ((), ())), preferred_element_type=jnp.float32
    )


def squares(block_part):
    widened = block_part.astype(jnp.float32)
    return jnp.sum(widened * widened, axis=1)


def moved(value, side, place):
    pairs = []
    for row in range(side):
        for col in range(side):
            to_row, to_col = place(row, col)
            pairs.append((row * side + col, to_row * side + to_col))
    return lax.ppermute(value, ("row", "col"), pairs)


def finish(summed, left_sq, right_sq, feat_total):
    left_scale = lax.rsqrt(left_sq / feat_total + epsilon)
    right_scale = lax.rsqrt(right_sq / feat_total + epsilon)
    return summed / feat_total * left_scale[:, None] * right_scale[None, :]


def on_square_grid(left_docs, right_docs):
    side = lax.axis_size("col")
    feat_total = left_docs.shape[1] * side
    row, col = lax.axis_index("row"), lax.axis_index("col")

    step_even = [
        moved(right_docs, side, lambda k, c, j=j: (c ^ (2 * j), k)) for j in range(side // 2)
    ]
    held = []
    for block in step_even:
        held.append(block)
        held.append(moved(block, side, lambda r, c: (r ^ 1, c)))
    left_own, right_own = squares(left_docs), squares(right_docs)
    left_sq, right_sq = left_own, right_own
    for delta in range(1, side):
        left_sq = left_sq + moved(left_own, side, lambda r, c, d=delta: (r, c ^ d))
        right_sq = right_sq + moved(right_own, side, lambda r, c, d=delta: (r ^ d, c))

    partial = jnp.stack([contract(left_docs, block) for block in held])

    def for_col(target):
        return lax.dynamic_index_in_dim(partial, row ^ target, 0, keepdims=False)

    summed = for_col(col)
    for delta in range(1, side):
        summed = summed + moved(for_col(col ^ delta), side, lambda r, c, d=delta: (r, c ^ d))
    return finish(summed, left_sq, right_sq, feat_total)


def on_any_grid(left_docs, right_docs):
    feat_total = left_docs.shape[1] * lax.axis_size("col")
    right_all = lax.all_gather(right_docs, "row", axis=1, tiled=True)
    held = lax.all_to_all(right_all, "col", split_axis=1, concat_axis=0, tiled=True)
    summed = lax.psum_scatter(contract(left_docs, held), "col", scatter_dimension=1, tiled=True)
    left_sq = lax.psum(squares(left_docs), "col")
    right_sq = lax.psum(squares(right_docs), "row")
    return finish(summed, left_sq, right_sq, feat_total)


def solution(mesh):
    side = mesh.shape["col"]
    square = mesh.shape["row"] == side and side >= 4 and side & (side - 1) == 0
    in_specs = (P(("bucket", "row"), "col"), P(("bucket", "col"), "row"))
    out_specs = P(("bucket", "row"), "col")
    return jax.shard_map(
        on_square_grid if square else on_any_grid,
        mesh=mesh, in_specs=in_specs, out_specs=out_specs, check_vma=False,
    )
```

```python
import jax
import jax.numpy as jnp
from jax import lax
from jax.sharding import PartitionSpec as P

epsilon = 1e-06


def contract(left_part, right_part):
    return lax.dot_general(
        left_part, right_part, (((1,), (1,)), ((), ())), preferred_element_type=jnp.float32
    )


def squares(block_part):
    widened = block_part.astype(jnp.float32)
    return jnp.sum(widened * widened, axis=1)


def moved(value, side, place):
    pairs = []
    for row in range(side):
        for col in range(side):
            to_row, to_col = place(row, col)
            pairs.append((row * side + col, to_row * side + to_col))
    return lax.ppermute(value, ("row", "col"), pairs)


def finish(summed, left_sq, right_sq, feat_total):
    left_scale = lax.rsqrt(left_sq / feat_total + epsilon)
    right_scale = lax.rsqrt(right_sq / feat_total + epsilon)
    return summed / feat_total * left_scale[:, None] * right_scale[None, :]


def on_square_grid(left_docs, right_docs):
    side = lax.axis_size("col")
    feat_total = left_docs.shape[1] * side
    row, col = lax.axis_index("row"), lax.axis_index("col")

    def spread(c):
        return 2 * (c & 1) + (c >> 1)

    held = moved(right_docs, side, lambda k, c: (spread(c), k))
    far = moved(left_docs, side, lambda r, c: (r ^ 2, c))
    near = moved(left_docs, side, lambda r, c: (r ^ 1, c))
    lefts = [left_docs, near, far, moved(far, side, lambda r, c: (r ^ 1, c))]
    partial = jnp.stack([contract(block, held) for block in lefts])

    summed = 0.0
    for m in range(side):
        mine = lax.dynamic_index_in_dim(partial, row ^ col ^ m, 0, keepdims=False)
        summed = summed + moved(mine, side, lambda i, k, m=m: (k ^ m, spread(i)))

    left_sq, right_sq = squares(left_docs), squares(right_docs)
    left_sq, right_sq, _ = lax.optimization_barrier((left_sq, right_sq, partial))
    for step in (1, 2):
        left_sq = left_sq + moved(left_sq, side, lambda r, c, d=step: (r, c ^ d))
        right_sq = right_sq + moved(right_sq, side, lambda r, c, d=step: (r ^ d, c))
    return finish(summed, left_sq, right_sq, feat_total)


def on_any_grid(left_docs, right_docs):
    feat_total = left_docs.shape[1] * lax.axis_size("col")
    right_all = lax.all_gather(right_docs, "row", axis=1, tiled=True)
    held = lax.all_to_all(right_all, "col", split_axis=1, concat_axis=0, tiled=True)
    summed = lax.psum_scatter(contract(left_docs, held), "col", scatter_dimension=1, tiled=True)
    left_sq = lax.psum(squares(left_docs), "col")
    right_sq = lax.psum(squares(right_docs), "row")
    return finish(summed, left_sq, right_sq, feat_total)


def solution(mesh):
    square = mesh.shape["row"] == mesh.shape["col"] == 4
    in_specs = (P(("bucket", "row"), "col"), P(("bucket", "col"), "row"))
    out_specs = P(("bucket", "row"), "col")
    return jax.shard_map(
        on_square_grid if square else on_any_grid,
        mesh=mesh, in_specs=in_specs, out_specs=out_specs, check_vma=False,
    )
```

```python
import jax
import jax.numpy as jnp
from jax import lax
from jax.sharding import PartitionSpec as P

epsilon = 1e-06


def contract(left_part, right_part):
    return lax.dot_general(
        left_part, right_part, (((1,), (1,)), ((), ())), preferred_element_type=jnp.float32
    )


def squares(block_part):
    widened = block_part.astype(jnp.float32)
    return jnp.sum(widened * widened, axis=1)


def moved(value, side, place):
    pairs = []
    for row in range(side):
        for col in range(side):
            to_row, to_col = place(row, col)
            pairs.append((row * side + col, to_row * side + to_col))
    return lax.ppermute(value, ("row", "col"), pairs)


def finish(summed, left_sq, right_sq, feat_total):
    left_scale = lax.rsqrt(left_sq / feat_total + epsilon)
    right_scale = lax.rsqrt(right_sq / feat_total + epsilon)
    return summed / feat_total * left_scale[:, None] * right_scale[None, :]


def on_square_grid(left_docs, right_docs):
    side = lax.axis_size("col")
    feat_total = left_docs.shape[1] * side
    row = lax.axis_index("row")

    step_even = [
        moved(right_docs, side, lambda k, c, j=j: (c ^ (2 * j), k)) for j in range(side // 2)
    ]
    held = []
    for block in step_even:
        held.append(block)
        held.append(moved(block, side, lambda r, c: (r ^ 1, c)))
    left_own, right_own = squares(left_docs), squares(right_docs)
    left_sq, right_sq = left_own, right_own
    for delta in range(1, side):
        left_sq = left_sq + moved(left_own, side, lambda r, c, d=delta: (r, c ^ d))
        right_sq = right_sq + moved(right_own, side, lambda r, c, d=delta: (r ^ d, c))

    partial = jnp.stack([contract(left_docs, block) for block in held])
    partial = jnp.stack(
        [lax.dynamic_index_in_dim(partial, row ^ c, 0, keepdims=False) for c in range(side)]
    )
    summed = jnp.sum(lax.all_to_all(partial, "col", split_axis=0, concat_axis=0), axis=0)
    return finish(summed, left_sq, right_sq, feat_total)


def on_any_grid(left_docs, right_docs):
    feat_total = left_docs.shape[1] * lax.axis_size("col")
    right_all = lax.all_gather(right_docs, "row", axis=1, tiled=True)
    held = lax.all_to_all(right_all, "col", split_axis=1, concat_axis=0, tiled=True)
    summed = lax.psum_scatter(contract(left_docs, held), "col", scatter_dimension=1, tiled=True)
    left_sq = lax.psum(squares(left_docs), "col")
    right_sq = lax.psum(squares(right_docs), "row")
    return finish(summed, left_sq, right_sq, feat_total)


def solution(mesh):
    side = mesh.shape["col"]
    square = mesh.shape["row"] == side and side >= 4 and side & (side - 1) == 0
    in_specs = (P(("bucket", "row"), "col"), P(("bucket", "col"), "row"))
    out_specs = P(("bucket", "row"), "col")
    return jax.shard_map(
        on_square_grid if square else on_any_grid,
        mesh=mesh, in_specs=in_specs, out_specs=out_specs, check_vma=False,
    )
```

```python
import functools

import jax
import jax.numpy as jnp
from jax import lax
from jax.experimental import pallas as pl
from jax.experimental.pallas import tpu as pltpu
from jax.sharding import PartitionSpec as P

epsilon = 1e-06


def contract(left_part, right_part):
    return lax.dot_general(
        left_part, right_part, (((1,), (1,)), ((), ())), preferred_element_type=jnp.float32
    )


def squares(block_part):
    widened = block_part.astype(jnp.float32)
    return jnp.sum(widened * widened, axis=1)


def moved(value, side, place):
    pairs = []
    for row in range(side):
        for col in range(side):
            target = place(row, col)
            if target is not None:
                pairs.append((row * side + col, target[0] * side + target[1]))
    return lax.ppermute(value, ("row", "col"), pairs)


def finish(summed, left_sq, right_sq, feat_total):
    left_scale = lax.rsqrt(left_sq / feat_total + epsilon)
    right_scale = lax.rsqrt(right_sq / feat_total + epsilon)
    return summed / feat_total * left_scale[:, None] * right_scale[None, :]


def row_squares(block):
    wide = block.astype(jnp.float32)
    wide = wide * wide
    high = wide.astype(jnp.bfloat16)
    low = (wide - high.astype(jnp.float32)).astype(jnp.bfloat16)
    ones = jnp.ones((8, block.shape[1]), jnp.bfloat16)
    return contract(ones, high) + contract(ones, low)


def multiply_kernel(turn, left, near, early_inner, late_inner, early_outer, late_outer, *messages):
    rows, width = left.shape[0], early_inner.shape[0]
    early = turn[0] == 1
    line = lax.broadcasted_iota(jnp.int32, (8, width), 0)
    lefts = [(block[...], row_squares(block[...])) for block in (left, near)]
    for v, (one, other) in enumerate(((early_outer, late_outer), (early_inner, late_inner))):
        right = jnp.where(early, one[...], other[...])
        right_sq = row_squares(right)
        for u, (block, left_sq) in enumerate(lefts):
            gram = contract(block, right)
            sums = right_sq
            for part in range(rows // width):
                sums = jnp.where(line == part + 1, left_sq[:, part * width:(part + 1) * width], sums)
            number = 2 * (v ^ turn[2]) + (u ^ turn[1])
            for n, message in enumerate(messages):
                @pl.when(number == n)
                def _(message=message, gram=gram, sums=sums):
                    message[:rows] = gram
                    message[rows:] = sums


def multiply(turn, left, *others):
    shape = (left.shape[0] + 8, others[-1].shape[0])
    return pl.pallas_call(
        multiply_kernel,
        out_shape=[jax.ShapeDtypeStruct(shape, jnp.float32)] * 4,
        in_specs=[pl.BlockSpec(memory_space=pltpu.SMEM)] + [pl.BlockSpec(memory_space=pltpu.VMEM)] * 6,
        out_specs=[pl.BlockSpec(memory_space=pltpu.VMEM)] * 4,
        compiler_params=pltpu.CompilerParams(vmem_limit_bytes=24 * 2**20),
    )(turn, left, *others)


def scale_kernel(feat_total, *refs):
    messages, out = refs[:-1], refs[-1]
    rows, width = out.shape
    total = messages[0][...]
    for message in messages[1:]:
        total = total + message[...]
    scales = lax.rsqrt(total[rows:] / feat_total + epsilon)
    tile = (width, width)
    diagonal = lax.broadcasted_iota(jnp.int32, tile, 0) == lax.broadcasted_iota(jnp.int32, tile, 1)
    for part in range(rows // width):
        along = jnp.broadcast_to(scales[part + 1:part + 2], tile)
        down = jnp.sum(jnp.where(diagonal, along, 0.0), axis=1, keepdims=True)
        here = slice(part * width, (part + 1) * width)
        out[here] = total[here] / feat_total * down * scales[:1]


def scale(feat_total, messages):
    rows, width = messages[0].shape
    return pl.pallas_call(
        functools.partial(scale_kernel, feat_total),
        out_shape=jax.ShapeDtypeStruct((rows - 8, width), jnp.float32),
        in_specs=[pl.BlockSpec(memory_space=pltpu.VMEM)] * len(messages),
        out_specs=pl.BlockSpec(memory_space=pltpu.VMEM),
    )(*messages)


def on_square_grid(left_docs, right_docs):
    side = lax.axis_size("col")
    feat_total = left_docs.shape[1] * side
    row, col = lax.axis_index("row"), lax.axis_index("col")
    core = row & 1
    early = (row >> 1) == (col >> 1)

    def inner(c):
        return c in (1, 2)

    def taker(r, c):
        return (r & 2) + (c & 1)

    crossed = moved(right_docs, side, lambda r, c: None if inner(c) else (r ^ 2, c))
    early_inner = moved(right_docs, side, lambda r, c: (taker(r, c), r) if inner(c) else None)
    early_outer = moved(right_docs, side, lambda r, c: None if inner(c) else (taker(r, c), r))
    near = moved(left_docs, side, lambda r, c: (r ^ 1, c))
    late_outer = moved(crossed, side, lambda r, c: None if inner(c) else (taker(r, c), r ^ 2))
    late_inner = moved(early_inner, side, lambda r, c: (r ^ 2, c) if r >> 1 == c >> 1 else None)
    turn = jnp.stack([early.astype(jnp.int32), (col & 1) ^ core, (col >> 1) ^ core])
    messages = multiply(turn, left_docs, near, early_inner, late_inner, early_outer, late_outer)
    received = [
        moved(
            messages[2 * cross + flip],
            side,
            lambda r, k, g=cross, f=flip: ((r & 2) + ((k & 1) ^ f), (r & 1) + 2 * ((k >> 1) ^ g)),
        )
        for cross in (0, 1)
        for flip in (0, 1)
    ]
    return scale(feat_total, received)


def on_any_grid(left_docs, right_docs):
    feat_total = left_docs.shape[1] * lax.axis_size("col")
    right_all = lax.all_gather(right_docs, "row", axis=1, tiled=True)
    held = lax.all_to_all(right_all, "col", split_axis=1, concat_axis=0, tiled=True)
    summed = lax.psum_scatter(contract(left_docs, held), "col", scatter_dimension=1, tiled=True)
    left_sq = lax.psum(squares(left_docs), "col")
    right_sq = lax.psum(squares(right_docs), "row")
    return finish(summed, left_sq, right_sq, feat_total)


def solution(mesh):
    square = mesh.shape["row"] == mesh.shape["col"] == 4
    in_specs = (P(("bucket", "row"), "col"), P(("bucket", "col"), "row"))
    out_specs = P(("bucket", "row"), "col")
    return jax.shard_map(
        on_square_grid if square else on_any_grid,
        mesh=mesh, in_specs=in_specs, out_specs=out_specs, check_vma=False,
    )
```

```python
import jax
import jax.numpy as jnp
from jax import lax
from jax.sharding import PartitionSpec as P

epsilon = 1e-06
top = 2.0**15


def inverse_norm(sum_of_squares):
    return lax.rsqrt(jnp.maximum(sum_of_squares, 1e-36))


def contract(left_part, right_part):
    return lax.dot_general(
        left_part, right_part, (((1,), (1,)), ((), ())), preferred_element_type=jnp.float32
    )


def squares(block_part):
    widened = block_part.astype(jnp.float32)
    return jnp.sum(widened * widened, axis=1)


def moved(value, side, place):
    pairs = []
    for row in range(side):
        for col in range(side):
            to_row, to_col = place(row, col)
            pairs.append((row * side + col, to_row * side + to_col))
    return lax.ppermute(value, ("row", "col"), pairs)


def finish(summed, left_sq, right_sq, feat_total):
    left_scale = lax.rsqrt(left_sq / feat_total + epsilon)
    right_scale = lax.rsqrt(right_sq / feat_total + epsilon)
    return summed / feat_total * left_scale[:, None] * right_scale[None, :]


def on_square_grid(left_docs, right_docs):
    side = lax.axis_size("col")
    feat_total = left_docs.shape[1] * side
    row, col = lax.axis_index("row"), lax.axis_index("col")
    x, p = row >> 1, row & 1

    first = moved(right_docs, side, lambda k, c: (2 * (c & 1) + (c >> 1), k))
    far = moved(left_docs, side, lambda r, c: (r ^ 2, c))

    left_sq, right_sq = squares(left_docs), squares(right_docs)
    left_sqs = jnp.stack([left_sq] + [moved(left_sq, side, lambda r, c, d=d: (r, c ^ d)) for d in range(1, side)])
    right_sqs = jnp.stack([right_sq] + [moved(right_sq, side, lambda r, c, d=d: (r ^ d, c)) for d in range(1, side)])

    second = moved(first, side, lambda r, c: (r ^ 1, c))

    def tile(left_block, right_block):
        gram = contract(left_block, right_block)
        down, along = inverse_norm(squares(left_block)), inverse_norm(squares(right_block))
        return (gram * (down * top)[:, None] * along[None, :]).astype(jnp.float16)

    tiles = jnp.stack([tile(l, r) for l in (left_docs, far) for r in (first, second)])
    left_scale = lax.rsqrt(jnp.sum(left_sqs, axis=0) / feat_total + epsilon)
    right_scale = lax.rsqrt(jnp.sum(right_sqs, axis=0) / feat_total + epsilon)
    similarity = 0.0
    for m in range(side):
        index = 2 * ((col >> 1) ^ (m >> 1) ^ x) + ((col & 1) ^ (m & 1) ^ p)
        mine = lax.dynamic_index_in_dim(tiles, index, 0, keepdims=False)
        got = moved(mine, side, lambda r, k, m=m: (((k ^ m) & 2) + (r & 1), (r >> 1) + 2 * ((k ^ m) & 1)))
        features = (2 * x + (col >> 1)) ^ m
        down = lax.dynamic_index_in_dim(left_sqs, features ^ col, 0, keepdims=False)
        along = lax.dynamic_index_in_dim(right_sqs, features ^ row, 0, keepdims=False)
        down = left_scale / (top * feat_total * inverse_norm(down))
        along = right_scale / inverse_norm(along)
        similarity = similarity + got.astype(jnp.float32) * down[:, None] * along[None, :]
    return similarity


def on_any_grid(left_docs, right_docs):
    feat_total = left_docs.shape[1] * lax.axis_size("col")
    right_all = lax.all_gather(right_docs, "row", axis=1, tiled=True)
    held = lax.all_to_all(right_all, "col", split_axis=1, concat_axis=0, tiled=True)
    summed = lax.psum_scatter(contract(left_docs, held), "col", scatter_dimension=1, tiled=True)
    left_sq = lax.psum(squares(left_docs), "col")
    right_sq = lax.psum(squares(right_docs), "row")
    return finish(summed, left_sq, right_sq, feat_total)


def solution(mesh):
    square = mesh.shape["row"] == mesh.shape["col"] == 4
    in_specs = (P(("bucket", "row"), "col"), P(("bucket", "col"), "row"))
    out_specs = P(("bucket", "row"), "col")
    return jax.shard_map(
        on_square_grid if square else on_any_grid,
        mesh=mesh, in_specs=in_specs, out_specs=out_specs, check_vma=False,
    )
```

```python
import jax
import jax.numpy as jnp
from jax import lax
from jax.sharding import PartitionSpec as P

epsilon = 1e-06
top = 2.0**15


def contract(left_part, right_part):
    return lax.dot_general(
        left_part, right_part, (((1,), (1,)), ((), ())), preferred_element_type=jnp.float32
    )


def squares(block_part):
    widened = block_part.astype(jnp.float32)
    return jnp.sum(widened * widened, axis=1)


def moved(value, side, place):
    pairs = []
    for row in range(side):
        for col in range(side):
            to_row, to_col = place(row, col)
            pairs.append((row * side + col, to_row * side + to_col))
    return lax.ppermute(value, ("row", "col"), pairs)


def finish(summed, left_sq, right_sq, feat_total):
    left_scale = lax.rsqrt(left_sq / feat_total + epsilon)
    right_scale = lax.rsqrt(right_sq / feat_total + epsilon)
    return summed / feat_total * left_scale[:, None] * right_scale[None, :]


def packed(sums):
    root = 16.0 * jnp.sqrt(jnp.sqrt(jnp.sqrt(jnp.maximum(sums, 1e-36))))
    high = lax.reduce_precision(root, 5, 10)
    low = lax.reduce_precision((root - high) * 1024.0, 5, 10)
    return high.astype(jnp.float16), low.astype(jnp.float16), unpacked(high, low)


def unpacked(high, low):
    root = (high + low / 1024.0) / 16.0
    for _ in range(3):
        root = root * root
    return root


def on_square_grid(left_docs, right_docs):
    side = lax.axis_size("col")
    feat_total = left_docs.shape[1] * side
    rows, width = left_docs.shape[0], right_docs.shape[0]

    far = moved(left_docs, side, lambda r, c: (r ^ 2, c))
    first = moved(right_docs, side, lambda k, c: (2 * ((k ^ c) & 1) + ((k ^ c) >> 1), k))
    second = moved(first, side, lambda r, c: (r ^ 1, c))

    def message(left_block, left_sums, right_block, right_sums):
        left_high, left_low, left_sq = left_sums
        right_high, right_low, right_sq = right_sums
        down, along = top * lax.rsqrt(left_sq), lax.rsqrt(right_sq)
        tile = (contract(left_block, right_block) * down[:, None] * along[None, :]).astype(jnp.float16)
        halves = (rows // width, width)
        sums = [left_high.reshape(halves), left_low.reshape(halves), right_high[None], right_low[None]]
        spare = -sum(part.shape[0] for part in sums) % 8
        return jnp.concatenate([tile, *sums, jnp.zeros((spare, width), jnp.float16)])

    received = []
    rights = [(block, packed(squares(block))) for block in (first, second)]
    for g, left_block in enumerate((left_docs, far)):
        left_sums = packed(squares(left_block))
        for j, (right_block, right_sums) in enumerate(rights):
            received.append(
                moved(
                    message(left_block, left_sums, right_block, right_sums),
                    side,
                    lambda r, k, g=g, j=j: (r ^ (2 * g), k ^ ((r >> 1) + 2 * ((r & 1) ^ j))),
                )
            )

    parts = []
    for got in received:
        wide = got.astype(jnp.float32)
        part = rows // width
        left_high, left_low, right_high, right_low = jnp.split(wide[rows:rows + 2 * part + 2], (part, 2 * part, 2 * part + 1))
        parts.append((wide[:rows], unpacked(left_high, left_low).reshape(rows), unpacked(right_high, right_low).reshape(width)))
    left_scale = lax.rsqrt(sum(part[1] for part in parts) / feat_total + epsilon) / (feat_total * top)
    right_scale = lax.rsqrt(sum(part[2] for part in parts) / feat_total + epsilon)
    return sum(
        tile * (left_scale * jnp.sqrt(left_sq))[:, None] * (right_scale * jnp.sqrt(right_sq))[None, :]
        for tile, left_sq, right_sq in parts
    )


def on_any_grid(left_docs, right_docs):
    feat_total = left_docs.shape[1] * lax.axis_size("col")
    right_all = lax.all_gather(right_docs, "row", axis=1, tiled=True)
    held = lax.all_to_all(right_all, "col", split_axis=1, concat_axis=0, tiled=True)
    summed = lax.psum_scatter(contract(left_docs, held), "col", scatter_dimension=1, tiled=True)
    left_sq = lax.psum(squares(left_docs), "col")
    right_sq = lax.psum(squares(right_docs), "row")
    return finish(summed, left_sq, right_sq, feat_total)


def solution(mesh):
    square = mesh.shape["row"] == mesh.shape["col"] == 4
    in_specs = (P(("bucket", "row"), "col"), P(("bucket", "col"), "row"))
    out_specs = P(("bucket", "row"), "col")
    return jax.shard_map(
        on_square_grid if square else on_any_grid,
        mesh=mesh, in_specs=in_specs, out_specs=out_specs, check_vma=False,
    )
```

```python
import jax
import jax.numpy as jnp
from jax import lax
from jax.sharding import PartitionSpec as P

epsilon = 1e-06
top = 2.0**15


def contract(left_part, right_part):
    return lax.dot_general(
        left_part, right_part, (((1,), (1,)), ((), ())), preferred_element_type=jnp.float32
    )


def squares(block_part):
    widened = block_part.astype(jnp.float32)
    return jnp.sum(widened * widened, axis=1)


def moved(value, side, place):
    pairs = []
    for row in range(side):
        for col in range(side):
            to_row, to_col = place(row, col)
            pairs.append((row * side + col, to_row * side + to_col))
    return lax.ppermute(value, ("row", "col"), pairs)


def finish(summed, left_sq, right_sq, feat_total):
    left_scale = lax.rsqrt(left_sq / feat_total + epsilon)
    right_scale = lax.rsqrt(right_sq / feat_total + epsilon)
    return summed / feat_total * left_scale[:, None] * right_scale[None, :]


def packed(sums):
    root = 16.0 * jnp.sqrt(jnp.sqrt(jnp.sqrt(jnp.maximum(sums, 1e-36))))
    high = lax.reduce_precision(root, 5, 10)
    low = lax.reduce_precision((root - high) * 1024.0, 5, 10)
    return high.astype(jnp.float16), low.astype(jnp.float16), unpacked(high, low)


def unpacked(high, low):
    root = (high + low / 1024.0) / 16.0
    for _ in range(3):
        root = root * root
    return root


def on_square_grid(left_docs, right_docs):
    side = lax.axis_size("col")
    feat_total = left_docs.shape[1] * side
    rows, width = left_docs.shape[0], right_docs.shape[0]

    far = moved(left_docs, side, lambda r, c: (r ^ 2, c))
    first = moved(right_docs, side, lambda k, c: (2 * ((k ^ c) & 1) + ((k ^ c) >> 1), k))
    second = moved(first, side, lambda r, c: (r ^ 1, c))

    def message(left_block, left_sums, right_block, right_sums):
        left_high, left_low, left_sq = left_sums
        right_high, right_low, right_sq = right_sums
        down, along = top * lax.rsqrt(left_sq), lax.rsqrt(right_sq)
        tile = (contract(left_block, right_block) * down[:, None] * along[None, :]).astype(jnp.float16)
        halves = (rows // width, width)
        sums = [left_high.reshape(halves), left_low.reshape(halves), right_high[None], right_low[None]]
        spare = -sum(part.shape[0] for part in sums) % 8
        return jnp.concatenate([tile, *sums, jnp.zeros((spare, width), jnp.float16)])

    def sent(value, g, j):
        return moved(value, side, lambda r, k: (r ^ (2 * g), k ^ ((r >> 1) + 2 * ((r & 1) ^ j))))

    right_sums = [packed(squares(block)) for block in (first, second)]
    own_sums = packed(squares(left_docs))
    own = [message(left_docs, own_sums, block, sums) for block, sums in zip((first, second), right_sums)]
    far, _ = lax.optimization_barrier((far, own[1]))
    far_sums = packed(squares(far))
    others = [message(far, far_sums, block, sums) for block, sums in zip((first, second), right_sums)]

    def taken(got):
        wide = got.astype(jnp.float32)
        part = rows // width
        left_high, left_low, right_high, right_low = jnp.split(wide[rows:rows + 2 * part + 2], (part, 2 * part, 2 * part + 1))
        left_sq, right_sq = unpacked(left_high, left_low).reshape(rows), unpacked(right_high, right_low).reshape(width)
        return wide[:rows] * jnp.sqrt(left_sq)[:, None] * jnp.sqrt(right_sq)[None, :], left_sq, right_sq

    def added(one, other):
        return [left + right for left, right in zip(one, other)]

    own_got, _ = lax.optimization_barrier(([sent(value, 0, j) for j, value in enumerate(own)], others))
    near_sum = added(*map(taken, own_got))
    far_got = [sent(value, 1, j) for j, value in enumerate(others)]
    near_sum, far_got = lax.optimization_barrier((near_sum, far_got))
    summed, left_sq, right_sq = added(near_sum, added(*map(taken, far_got)))
    return finish(summed / top, left_sq, right_sq, feat_total)


def on_any_grid(left_docs, right_docs):
    feat_total = left_docs.shape[1] * lax.axis_size("col")
    right_all = lax.all_gather(right_docs, "row", axis=1, tiled=True)
    held = lax.all_to_all(right_all, "col", split_axis=1, concat_axis=0, tiled=True)
    summed = lax.psum_scatter(contract(left_docs, held), "col", scatter_dimension=1, tiled=True)
    left_sq = lax.psum(squares(left_docs), "col")
    right_sq = lax.psum(squares(right_docs), "row")
    return finish(summed, left_sq, right_sq, feat_total)


def solution(mesh):
    square = mesh.shape["row"] == mesh.shape["col"] == 4
    in_specs = (P(("bucket", "row"), "col"), P(("bucket", "col"), "row"))
    out_specs = P(("bucket", "row"), "col")
    return jax.shard_map(
        on_square_grid if square else on_any_grid,
        mesh=mesh, in_specs=in_specs, out_specs=out_specs, check_vma=False,
    )
```

```python
import jax
import jax.numpy as jnp
from jax import lax
from jax.sharding import PartitionSpec as P

epsilon = 1e-06
top = 2.0**15


def contract(left_part, right_part):
    return lax.dot_general(
        left_part, right_part, (((1,), (1,)), ((), ())), preferred_element_type=jnp.float32
    )


def squares(block_part):
    widened = block_part.astype(jnp.float32)
    return jnp.sum(widened * widened, axis=1)


def moved(value, side, place):
    pairs = []
    for row in range(side):
        for col in range(side):
            target = place(row, col)
            if target is not None:
                pairs.append((row * side + col, target[0] * side + target[1]))
    return lax.ppermute(value, ("row", "col"), pairs)


def finish(summed, left_sq, right_sq, feat_total):
    left_scale = lax.rsqrt(left_sq / feat_total + epsilon)
    right_scale = lax.rsqrt(right_sq / feat_total + epsilon)
    return summed / feat_total * left_scale[:, None] * right_scale[None, :]


def packed(sums):
    root = 16.0 * jnp.sqrt(jnp.sqrt(jnp.sqrt(jnp.maximum(sums, 1e-36))))
    high = lax.reduce_precision(root, 5, 10)
    low = lax.reduce_precision((root - high) * 1024.0, 5, 10)
    return high.astype(jnp.float16), low.astype(jnp.float16), unpacked(high, low)


def unpacked(high, low):
    root = (high + low / 1024.0) / 16.0
    for _ in range(3):
        root = root * root
    return root


def on_square_grid(left_docs, right_docs):
    side = lax.axis_size("col")
    feat_total = left_docs.shape[1] * side
    rows, width = left_docs.shape[0], right_docs.shape[0]

    def taker(k, c):
        return 2 * ((k ^ c) & 1) + ((k ^ c) >> 1)

    def turns(k, c):
        return (k ^ c) >> 1 == 1 and (k ^ c) & 1 != k >> 1

    turned = moved(right_docs, side, lambda k, c: (k ^ 2, c) if turns(k, c) else None)
    far = moved(left_docs, side, lambda r, c: (r ^ 2, c))
    straight = moved(right_docs, side, lambda k, c: None if turns(k, c) else (taker(k, c), k))
    turned = moved(turned, side, lambda r, c: (taker(r ^ 2, c), r ^ 2) if turns(r ^ 2, c) else None)
    row, col = lax.axis_index("row"), lax.axis_index("col")
    first = jnp.where(((row & 1) == 1) & ((row >> 1) != (col >> 1)), turned, straight)
    first = lax.optimization_barrier(first)
    second = moved(first, side, lambda r, c: (r ^ 1, c))

    def message(left_block, left_sums, right_block, right_sums):
        left_high, left_low, left_sq = left_sums
        right_high, right_low, right_sq = right_sums
        down, along = top * lax.rsqrt(left_sq), lax.rsqrt(right_sq)
        tile = (contract(left_block, right_block) * down[:, None] * along[None, :]).astype(jnp.float16)
        halves = (rows // width, width)
        sums = [left_high.reshape(halves), left_low.reshape(halves), right_high[None], right_low[None]]
        spare = -sum(part.shape[0] for part in sums) % 8
        return jnp.concatenate([tile, *sums, jnp.zeros((spare, width), jnp.float16)])

    def sent(value, g, j):
        return moved(value, side, lambda r, k: (r ^ (2 * g), k ^ ((r >> 1) + 2 * ((r & 1) ^ j))))

    right_sums = [packed(squares(block)) for block in (first, second)]
    own_sums = packed(squares(left_docs))
    own = [message(left_docs, own_sums, block, sums) for block, sums in zip((first, second), right_sums)]
    far, _ = lax.optimization_barrier((far, own[1]))
    far_sums = packed(squares(far))
    others = [message(far, far_sums, block, sums) for block, sums in zip((first, second), right_sums)]

    def taken(got):
        wide = got.astype(jnp.float32)
        part = rows // width
        left_high, left_low, right_high, right_low = jnp.split(wide[rows:rows + 2 * part + 2], (part, 2 * part, 2 * part + 1))
        left_sq, right_sq = unpacked(left_high, left_low).reshape(rows), unpacked(right_high, right_low).reshape(width)
        return wide[:rows] * jnp.sqrt(left_sq)[:, None] * jnp.sqrt(right_sq)[None, :], left_sq, right_sq

    def added(one, other):
        return [left + right for left, right in zip(one, other)]

    own_got, _ = lax.optimization_barrier(([sent(value, 0, j) for j, value in enumerate(own)], others))
    near_sum = added(*map(taken, own_got))
    far_got = [sent(value, 1, j) for j, value in enumerate(others)]
    near_sum, far_got = lax.optimization_barrier((near_sum, far_got))
    summed, left_sq, right_sq = added(near_sum, added(*map(taken, far_got)))
    return finish(summed / top, left_sq, right_sq, feat_total)


def on_any_grid(left_docs, right_docs):
    feat_total = left_docs.shape[1] * lax.axis_size("col")
    right_all = lax.all_gather(right_docs, "row", axis=1, tiled=True)
    held = lax.all_to_all(right_all, "col", split_axis=1, concat_axis=0, tiled=True)
    summed = lax.psum_scatter(contract(left_docs, held), "col", scatter_dimension=1, tiled=True)
    left_sq = lax.psum(squares(left_docs), "col")
    right_sq = lax.psum(squares(right_docs), "row")
    return finish(summed, left_sq, right_sq, feat_total)


def solution(mesh):
    square = mesh.shape["row"] == mesh.shape["col"] == 4
    in_specs = (P(("bucket", "row"), "col"), P(("bucket", "col"), "row"))
    out_specs = P(("bucket", "row"), "col")
    return jax.shard_map(
        on_square_grid if square else on_any_grid,
        mesh=mesh, in_specs=in_specs, out_specs=out_specs, check_vma=False,
    )
```

```python
import jax
import jax.numpy as jnp
from jax import lax
from jax.sharding import PartitionSpec as P

epsilon = 1e-06
top = 2.0**15


def contract(left_part, right_part):
    return lax.dot_general(
        left_part, right_part, (((1,), (1,)), ((), ())), preferred_element_type=jnp.float32
    )


def squares(block_part):
    widened = block_part.astype(jnp.float32)
    return jnp.sum(widened * widened, axis=1)


def moved(value, side, place):
    pairs = []
    for row in range(side):
        for col in range(side):
            to_row, to_col = place(row, col)
            pairs.append((row * side + col, to_row * side + to_col))
    return lax.ppermute(value, ("row", "col"), pairs)


def finish(summed, left_sq, right_sq, feat_total):
    left_scale = lax.rsqrt(left_sq / feat_total + epsilon)
    right_scale = lax.rsqrt(right_sq / feat_total + epsilon)
    return summed / feat_total * left_scale[:, None] * right_scale[None, :]


def packed(sums):
    root = 16.0 * jnp.sqrt(jnp.sqrt(jnp.sqrt(jnp.maximum(sums, 1e-36))))
    high = lax.reduce_precision(root, 5, 10)
    low = lax.reduce_precision((root - high) * 1024.0, 5, 10)
    return high.astype(jnp.float16), low.astype(jnp.float16), unpacked(high, low)


def unpacked(high, low):
    root = (high + low / 1024.0) / 16.0
    for _ in range(3):
        root = root * root
    return root


def on_square_grid(left_docs, right_docs):
    side = lax.axis_size("col")
    feat_total = left_docs.shape[1] * side
    rows, width = left_docs.shape[0], right_docs.shape[0]

    far = moved(left_docs, side, lambda r, c: (r ^ 2, c))
    first = moved(right_docs, side, lambda k, c: (2 * ((k ^ c) & 1) + ((k ^ c) >> 1), k))
    second = moved(first, side, lambda r, c: (r ^ 1, c))

    def message(left_block, left_sums, right_block, right_sums):
        left_high, left_low, left_sq = left_sums
        right_high, right_low, right_sq = right_sums
        down, along = top * lax.rsqrt(left_sq), lax.rsqrt(right_sq)
        tile = (contract(left_block, right_block) * down[:, None] * along[None, :]).astype(jnp.float16)
        halves = (rows // width, width)
        sums = [left_high.reshape(halves), left_low.reshape(halves), right_high[None], right_low[None]]
        spare = -sum(part.shape[0] for part in sums) % 8
        return jnp.concatenate([tile, *sums, jnp.zeros((spare, width), jnp.float16)])

    def sent(value, g, j):
        return moved(value, side, lambda r, k: (r ^ (2 * g), k ^ ((r >> 1) + 2 * ((r & 1) ^ j))))

    right_sums = [packed(squares(block)) for block in (first, second)]
    own_sums = packed(squares(left_docs))
    own = [message(left_docs, own_sums, block, sums) for block, sums in zip((first, second), right_sums)]
    far, _ = lax.optimization_barrier((far, own[1]))
    far_sums = packed(squares(far))
    others = [message(far, far_sums, block, sums) for block, sums in zip((first, second), right_sums)]

    def taken(got):
        wide = got.astype(jnp.float32)
        part = rows // width
        left_high, left_low, right_high, right_low = jnp.split(wide[rows:rows + 2 * part + 2], (part, 2 * part, 2 * part + 1))
        left_sq, right_sq = unpacked(left_high, left_low).reshape(rows), unpacked(right_high, right_low).reshape(width)
        return wide[:rows] * jnp.sqrt(left_sq)[:, None] * jnp.sqrt(right_sq)[None, :], left_sq, right_sq

    def added(one, other):
        return [left + right for left, right in zip(one, other)]

    own_got, _ = lax.optimization_barrier(([sent(value, 0, j) for j, value in enumerate(own)], others))
    near_sum = added(*map(taken, own_got))
    far_got = [sent(value, 1, j) for j, value in enumerate(others)]
    summed, left_sq, right_sq = added(near_sum, added(*map(taken, far_got)))
    return finish(summed / top, left_sq, right_sq, feat_total)


def on_any_grid(left_docs, right_docs):
    feat_total = left_docs.shape[1] * lax.axis_size("col")
    right_all = lax.all_gather(right_docs, "row", axis=1, tiled=True)
    held = lax.all_to_all(right_all, "col", split_axis=1, concat_axis=0, tiled=True)
    summed = lax.psum_scatter(contract(left_docs, held), "col", scatter_dimension=1, tiled=True)
    left_sq = lax.psum(squares(left_docs), "col")
    right_sq = lax.psum(squares(right_docs), "row")
    return finish(summed, left_sq, right_sq, feat_total)


def solution(mesh):
    square = mesh.shape["row"] == mesh.shape["col"] == 4
    in_specs = (P(("bucket", "row"), "col"), P(("bucket", "col"), "row"))
    out_specs = P(("bucket", "row"), "col")
    return jax.shard_map(
        on_square_grid if square else on_any_grid,
        mesh=mesh, in_specs=in_specs, out_specs=out_specs, check_vma=False,
    )
```

```python
import jax
import jax.numpy as jnp
from jax import lax
from jax.sharding import PartitionSpec as P

epsilon = 1e-06


def contract(left_part, right_part):
    return lax.dot_general(
        left_part, right_part, (((1,), (1,)), ((), ())), preferred_element_type=jnp.float32
    )


def squares(block_part):
    widened = block_part.astype(jnp.float32)
    return jnp.sum(widened * widened, axis=1)


def moved(value, side, place):
    pairs = []
    for row in range(side):
        for col in range(side):
            target = place(row, col)
            if target is not None:
                pairs.append((row * side + col, target[0] * side + target[1]))
    return lax.ppermute(value, ("row", "col"), pairs)


def finish(summed, left_sq, right_sq, feat_total):
    left_scale = lax.rsqrt(left_sq / feat_total + epsilon)
    right_scale = lax.rsqrt(right_sq / feat_total + epsilon)
    return summed / feat_total * left_scale[:, None] * right_scale[None, :]


def on_square_grid(left_docs, right_docs):
    side = lax.axis_size("col")
    feat_total = left_docs.shape[1] * side
    rows, width = left_docs.shape[0], right_docs.shape[0]
    row, col = lax.axis_index("row"), lax.axis_index("col")
    at_home = (row >> 1) == (col >> 1)
    same = (row & 1) == (col & 1)

    def other_core(block):
        return moved(block, side, lambda r, c: (r ^ 1, c))

    swapped = moved(right_docs, side, lambda r, c: (r ^ 2, c))
    left_other = moved(left_docs, side, lambda r, c: (r, c ^ 1))
    near, leaving = lax.optimization_barrier(
        (jnp.where(at_home, right_docs, swapped), jnp.where(at_home, swapped, right_docs))
    )
    cross = moved(leaving, side, lambda r, c: (r, c ^ 2))
    lefts = lax.optimization_barrier((jnp.where(same, left_docs, left_other), jnp.where(same, left_other, left_docs)))

    def half_sum(mine):
        blocks = (mine, other_core(mine))
        gram = sum(contract(left, right) for left, right in zip(lefts, blocks))
        return gram, sum(squares(block) for block in blocks)

    near_gram, near_sq = half_sum(near)
    cross_gram, cross_sq = half_sum(cross)
    left_sq = squares(left_docs) + squares(left_other)

    parts = rows // width
    sums = [cross_sq[None], left_sq.reshape(parts, width), jnp.zeros((-(parts + 1) % 8, width), jnp.float32)]
    got = moved(jnp.concatenate([cross_gram, *sums]), side, lambda r, c: (r, c ^ 2))
    left_sq = left_sq + got[rows + 1:rows + 1 + parts].reshape(rows)
    return finish(near_gram + got[:rows], left_sq, near_sq + got[rows], feat_total)


def on_any_grid(left_docs, right_docs):
    feat_total = left_docs.shape[1] * lax.axis_size("col")
    right_all = lax.all_gather(right_docs, "row", axis=1, tiled=True)
    held = lax.all_to_all(right_all, "col", split_axis=1, concat_axis=0, tiled=True)
    summed = lax.psum_scatter(contract(left_docs, held), "col", scatter_dimension=1, tiled=True)
    left_sq = lax.psum(squares(left_docs), "col")
    right_sq = lax.psum(squares(right_docs), "row")
    return finish(summed, left_sq, right_sq, feat_total)


def solution(mesh):
    square = mesh.shape["row"] == mesh.shape["col"] == 4
    in_specs = (P(("bucket", "row"), "col"), P(("bucket", "col"), "row"))
    out_specs = P(("bucket", "row"), "col")
    return jax.shard_map(
        on_square_grid if square else on_any_grid,
        mesh=mesh, in_specs=in_specs, out_specs=out_specs, check_vma=False,
    )
```

```python
import jax
import jax.numpy as jnp
from jax import lax
from jax.sharding import PartitionSpec as P

epsilon = 1e-06


def contract(left_part, right_part):
    return lax.dot_general(
        left_part, right_part, (((1,), (1,)), ((), ())), preferred_element_type=jnp.float32
    )


def squares(block_part):
    widened = block_part.astype(jnp.float32)
    return jnp.sum(widened * widened, axis=1)


def moved(value, side, place):
    pairs = []
    for row in range(side):
        for col in range(side):
            target = place(row, col)
            if target is not None:
                pairs.append((row * side + col, target[0] * side + target[1]))
    return lax.ppermute(value, ("row", "col"), pairs)


def finish(summed, left_sq, right_sq, feat_total):
    left_scale = lax.rsqrt(left_sq / feat_total + epsilon)
    right_scale = lax.rsqrt(right_sq / feat_total + epsilon)
    return summed / feat_total * left_scale[:, None] * right_scale[None, :]


def on_square_grid(left_docs, right_docs):
    side = lax.axis_size("col")
    feat_total = left_docs.shape[1] * side
    rows, width = left_docs.shape[0], right_docs.shape[0]
    row, col = lax.axis_index("row"), lax.axis_index("col")
    at_home = (row >> 1) == (col >> 1)
    same = (row & 1) == (col & 1)

    def other_core(block):
        return moved(block, side, lambda r, c: (r ^ 1, c))

    def home(r, c):
        return r >> 1 == c >> 1

    first, second = right_docs[:width // 2], right_docs[width // 2:]
    turned = moved(second, side, lambda r, c: None if home(r, c) else (r ^ 2, c))
    straight = moved(first, side, lambda r, c: None if home(r, c) else (r, c ^ 2))
    near = moved(right_docs, side, lambda r, c: (r ^ 2, c) if home(r, c) else None)
    left_other = moved(left_docs, side, lambda r, c: (r, c ^ 1))
    turned = moved(turned, side, lambda r, c: (r, c ^ 2) if home(r, c) else None)
    near = lax.optimization_barrier(jnp.where(at_home, right_docs, near))
    mine = lax.optimization_barrier(jnp.where(at_home, straight, turned))
    other = moved(mine, side, lambda r, c: (r ^ 2, c))
    cross = jnp.concatenate([jnp.where(at_home, mine, other), jnp.where(at_home, other, mine)])
    cross = lax.optimization_barrier(cross)
    lefts = lax.optimization_barrier((jnp.where(same, left_docs, left_other), jnp.where(same, left_other, left_docs)))

    def half_sum(mine):
        blocks = (mine, other_core(mine))
        gram = sum(contract(left, right) for left, right in zip(lefts, blocks))
        return gram, sum(squares(block) for block in blocks)

    near_gram, near_sq = half_sum(near)
    cross_gram, cross_sq = half_sum(cross)
    left_sq = squares(left_docs) + squares(left_other)

    parts = rows // width
    sums = [cross_sq[None], left_sq.reshape(parts, width), jnp.zeros((-(parts + 1) % 8, width), jnp.float32)]
    got = moved(jnp.concatenate([cross_gram, *sums]), side, lambda r, c: (r, c ^ 2))
    left_sq = left_sq + got[rows + 1:rows + 1 + parts].reshape(rows)
    return finish(near_gram + got[:rows], left_sq, near_sq + got[rows], feat_total)


def on_any_grid(left_docs, right_docs):
    feat_total = left_docs.shape[1] * lax.axis_size("col")
    right_all = lax.all_gather(right_docs, "row", axis=1, tiled=True)
    held = lax.all_to_all(right_all, "col", split_axis=1, concat_axis=0, tiled=True)
    summed = lax.psum_scatter(contract(left_docs, held), "col", scatter_dimension=1, tiled=True)
    left_sq = lax.psum(squares(left_docs), "col")
    right_sq = lax.psum(squares(right_docs), "row")
    return finish(summed, left_sq, right_sq, feat_total)


def solution(mesh):
    square = mesh.shape["row"] == mesh.shape["col"] == 4
    in_specs = (P(("bucket", "row"), "col"), P(("bucket", "col"), "row"))
    out_specs = P(("bucket", "row"), "col")
    return jax.shard_map(
        on_square_grid if square else on_any_grid,
        mesh=mesh, in_specs=in_specs, out_specs=out_specs, check_vma=False,
    )
```

```python
import jax
import jax.numpy as jnp
from jax import lax
from jax.sharding import PartitionSpec as P

epsilon = 1e-06


def contract(left_part, right_part):
    return lax.dot_general(
        left_part, right_part, (((1,), (1,)), ((), ())), preferred_element_type=jnp.float32
    )


def squares(block_part):
    widened = block_part.astype(jnp.float32)
    return jnp.sum(widened * widened, axis=1)


def moved(value, side, place):
    pairs = []
    for row in range(side):
        for col in range(side):
            target = place(row, col)
            if target is not None:
                pairs.append((row * side + col, target[0] * side + target[1]))
    return lax.ppermute(value, ("row", "col"), pairs)


def finish(summed, left_sq, right_sq, feat_total):
    left_scale = lax.rsqrt(left_sq / feat_total + epsilon)
    right_scale = lax.rsqrt(right_sq / feat_total + epsilon)
    return summed / feat_total * left_scale[:, None] * right_scale[None, :]


def on_square_grid(left_docs, right_docs):
    side = lax.axis_size("col")
    feat_total = left_docs.shape[1] * side
    rows, width = left_docs.shape[0], right_docs.shape[0]
    row, col = lax.axis_index("row"), lax.axis_index("col")
    at_home = (row >> 1) == (col >> 1)
    same = (row & 1) == (col & 1)

    def other_core(block):
        return moved(block, side, lambda r, c: (r ^ 1, c))

    nears, crosses = [], []
    for half in (right_docs[:width // 2], right_docs[width // 2:]):
        swapped = moved(half, side, lambda r, c: (r ^ 2, c))
        near, leaving = lax.optimization_barrier((jnp.where(at_home, half, swapped), jnp.where(at_home, swapped, half)))
        nears.append(near)
        crosses.append(moved(leaving, side, lambda r, c: (r, c ^ 2)))
    left_other = moved(left_docs, side, lambda r, c: (r, c ^ 1))
    near, cross = lax.optimization_barrier(jnp.concatenate(nears)), lax.optimization_barrier(jnp.concatenate(crosses))
    lefts = lax.optimization_barrier((jnp.where(same, left_docs, left_other), jnp.where(same, left_other, left_docs)))

    def half_sum(mine):
        blocks = (mine, other_core(mine))
        gram = sum(contract(left, right) for left, right in zip(lefts, blocks))
        return gram, sum(squares(block) for block in blocks)

    near_gram, near_sq = half_sum(near)
    cross_gram, cross_sq = half_sum(cross)
    left_sq = squares(left_docs) + squares(left_other)

    parts = rows // width
    sums = [cross_sq[None], left_sq.reshape(parts, width), jnp.zeros((-(parts + 1) % 8, width), jnp.float32)]
    got = moved(jnp.concatenate([cross_gram, *sums]), side, lambda r, c: (r, c ^ 2))
    left_sq = left_sq + got[rows + 1:rows + 1 + parts].reshape(rows)
    return finish(near_gram + got[:rows], left_sq, near_sq + got[rows], feat_total)


def on_any_grid(left_docs, right_docs):
    feat_total = left_docs.shape[1] * lax.axis_size("col")
    right_all = lax.all_gather(right_docs, "row", axis=1, tiled=True)
    held = lax.all_to_all(right_all, "col", split_axis=1, concat_axis=0, tiled=True)
    summed = lax.psum_scatter(contract(left_docs, held), "col", scatter_dimension=1, tiled=True)
    left_sq = lax.psum(squares(left_docs), "col")
    right_sq = lax.psum(squares(right_docs), "row")
    return finish(summed, left_sq, right_sq, feat_total)


def solution(mesh):
    square = mesh.shape["row"] == mesh.shape["col"] == 4
    in_specs = (P(("bucket", "row"), "col"), P(("bucket", "col"), "row"))
    out_specs = P(("bucket", "row"), "col")
    return jax.shard_map(
        on_square_grid if square else on_any_grid,
        mesh=mesh, in_specs=in_specs, out_specs=out_specs, check_vma=False,
    )
```

```python
import jax
import jax.numpy as jnp
from jax import lax
from jax.sharding import PartitionSpec as P

epsilon = 1e-06
top = 2.0**15


def contract(left_part, right_part):
    return lax.dot_general(
        left_part, right_part, (((1,), (1,)), ((), ())), preferred_element_type=jnp.float32
    )


def squares(block_part):
    widened = block_part.astype(jnp.float32)
    return jnp.sum(widened * widened, axis=1)


def moved(value, side, place):
    pairs = []
    for row in range(side):
        for col in range(side):
            target = place(row, col)
            if target is not None:
                pairs.append((row * side + col, target[0] * side + target[1]))
    return lax.ppermute(value, ("row", "col"), pairs)


def finish(summed, left_sq, right_sq, feat_total):
    left_scale = lax.rsqrt(left_sq / feat_total + epsilon)
    right_scale = lax.rsqrt(right_sq / feat_total + epsilon)
    return summed / feat_total * left_scale[:, None] * right_scale[None, :]


def packed(sums):
    root = 16.0 * jnp.sqrt(jnp.sqrt(jnp.sqrt(jnp.maximum(sums, 1e-36))))
    high = lax.reduce_precision(root, 5, 10)
    low = lax.reduce_precision((root - high) * 1024.0, 5, 10)
    return high.astype(jnp.float16), low.astype(jnp.float16), unpacked(high, low)


def unpacked(high, low):
    root = (high + low / 1024.0) / 16.0
    for _ in range(3):
        root = root * root
    return root


def on_square_grid(left_docs, right_docs):
    side = lax.axis_size("col")
    feat_total = left_docs.shape[1] * side
    rows, width = left_docs.shape[0], right_docs.shape[0]
    row, col = lax.axis_index("row"), lax.axis_index("col")
    at_home = (row >> 1) == (col >> 1)
    same = (row & 1) == (col & 1)

    def other_core(block):
        return moved(block, side, lambda r, c: (r ^ 1, c))

    nears, crosses = [], []
    for half in (right_docs[:width // 2], right_docs[width // 2:]):
        swapped = moved(half, side, lambda r, c: (r ^ 2, c))
        near, leaving = lax.optimization_barrier((jnp.where(at_home, half, swapped), jnp.where(at_home, swapped, half)))
        nears.append(near)
        crosses.append(moved(leaving, side, lambda r, c: (r, c ^ 2)))
    left_other = moved(left_docs, side, lambda r, c: (r, c ^ 1))
    near, cross = lax.optimization_barrier(jnp.concatenate(nears)), lax.optimization_barrier(jnp.concatenate(crosses))
    lefts = lax.optimization_barrier((jnp.where(same, left_docs, left_other), jnp.where(same, left_other, left_docs)))

    def half_sum(mine):
        blocks = (mine, other_core(mine))
        gram = sum(contract(left, right) for left, right in zip(lefts, blocks))
        return gram, sum(squares(block) for block in blocks)

    near_gram, near_sq = half_sum(near)
    cross_gram, cross_sq = half_sum(cross)
    left_sq = squares(left_docs) + squares(left_other)

    left_high, left_low, left_read = packed(left_sq)
    right_high, right_low, right_read = packed(cross_sq)
    tile = cross_gram * (top * lax.rsqrt(left_read))[:, None] * lax.rsqrt(right_read)[None, :]
    parts = rows // width
    sums = [left_high.reshape(parts, width), left_low.reshape(parts, width), right_high[None], right_low[None]]
    spare = jnp.zeros((-(2 * parts + 2) % 8, width), jnp.float16)
    got = moved(jnp.concatenate([tile.astype(jnp.float16), *sums, spare]), side, lambda r, c: (r, c ^ 2))

    got = got.astype(jnp.float32)
    sums = jnp.split(got[rows:rows + 2 * parts + 2], (parts, 2 * parts, 2 * parts + 1))
    left_got, right_got = unpacked(*sums[:2]).reshape(rows), unpacked(*sums[2:]).reshape(width)
    far_gram = got[:rows] * (jnp.sqrt(left_got) / top)[:, None] * jnp.sqrt(right_got)[None, :]
    return finish(near_gram + far_gram, left_sq + left_got, near_sq + right_got, feat_total)


def on_any_grid(left_docs, right_docs):
    feat_total = left_docs.shape[1] * lax.axis_size("col")
    right_all = lax.all_gather(right_docs, "row", axis=1, tiled=True)
    held = lax.all_to_all(right_all, "col", split_axis=1, concat_axis=0, tiled=True)
    summed = lax.psum_scatter(contract(left_docs, held), "col", scatter_dimension=1, tiled=True)
    left_sq = lax.psum(squares(left_docs), "col")
    right_sq = lax.psum(squares(right_docs), "row")
    return finish(summed, left_sq, right_sq, feat_total)


def solution(mesh):
    square = mesh.shape["row"] == mesh.shape["col"] == 4
    in_specs = (P(("bucket", "row"), "col"), P(("bucket", "col"), "row"))
    out_specs = P(("bucket", "row"), "col")
    return jax.shard_map(
        on_square_grid if square else on_any_grid,
        mesh=mesh, in_specs=in_specs, out_specs=out_specs, check_vma=False,
    )
```

```python
import jax
import jax.numpy as jnp
from jax import lax
from jax.sharding import PartitionSpec as P

epsilon = 1e-06
top = 2.0**15


def contract(left_part, right_part):
    return lax.dot_general(
        left_part, right_part, (((1,), (1,)), ((), ())), preferred_element_type=jnp.float32
    )


def squares(block_part):
    widened = block_part.astype(jnp.float32)
    return jnp.sum(widened * widened, axis=1)


def moved(value, side, place):
    pairs = []
    for row in range(side):
        for col in range(side):
            target = place(row, col)
            if target is not None:
                pairs.append((row * side + col, target[0] * side + target[1]))
    return lax.ppermute(value, ("row", "col"), pairs)


def finish(summed, left_sq, right_sq, feat_total):
    left_scale = lax.rsqrt(left_sq / feat_total + epsilon)
    right_scale = lax.rsqrt(right_sq / feat_total + epsilon)
    return summed / feat_total * left_scale[:, None] * right_scale[None, :]


def packed(sums):
    root = 16.0 * jnp.sqrt(jnp.sqrt(jnp.sqrt(jnp.maximum(sums, 1e-36))))
    high = lax.reduce_precision(root, 5, 10)
    low = lax.reduce_precision((root - high) * 1024.0, 5, 10)
    return high.astype(jnp.float16), low.astype(jnp.float16), unpacked(high, low)


def unpacked(high, low):
    root = (high + low / 1024.0) / 16.0
    for _ in range(3):
        root = root * root
    return root


def on_square_grid(left_docs, right_docs):
    side = lax.axis_size("col")
    feat_total = left_docs.shape[1] * side
    rows, width = left_docs.shape[0], right_docs.shape[0]
    row, col = lax.axis_index("row"), lax.axis_index("col")
    at_home = (row >> 1) == (col >> 1)
    same = (row & 1) == (col & 1)

    def other_core(block):
        return moved(block, side, lambda r, c: (r ^ 1, c))

    def over_x(block):
        return moved(block, side, lambda r, c: (r ^ 2, c))

    def over_middle(block):
        return moved(block, side, lambda r, c: (r, c ^ 2))

    part = width * 5 // 8
    swapped = over_x(right_docs)
    arrived = over_middle(right_docs[:part])
    left_other = moved(left_docs, side, lambda r, c: (r, c ^ 1))
    near, leaving = lax.optimization_barrier(
        (jnp.where(at_home, right_docs, swapped), jnp.where(at_home, swapped[part:], right_docs[part:]))
    )
    arrived, _ = lax.optimization_barrier((arrived, leaving))
    cross = jnp.concatenate([jnp.where(at_home, arrived, over_x(arrived)), over_middle(leaving)])
    cross = lax.optimization_barrier(cross)
    lefts = lax.optimization_barrier((jnp.where(same, left_docs, left_other), jnp.where(same, left_other, left_docs)))

    def half_sum(mine):
        blocks = (mine, other_core(mine))
        gram = sum(contract(left, right) for left, right in zip(lefts, blocks))
        return gram, sum(squares(block) for block in blocks)

    near_gram, near_sq = half_sum(near)
    cross_gram, cross_sq = half_sum(cross)
    left_sq = squares(left_docs) + squares(left_other)

    left_high, left_low, left_read = packed(left_sq)
    right_high, right_low, right_read = packed(cross_sq)
    tile = cross_gram * (top * lax.rsqrt(left_read))[:, None] * lax.rsqrt(right_read)[None, :]
    parts = rows // width
    sums = [left_high.reshape(parts, width), left_low.reshape(parts, width), right_high[None], right_low[None]]
    spare = jnp.zeros((-(2 * parts + 2) % 8, width), jnp.float16)
    got = moved(jnp.concatenate([tile.astype(jnp.float16), *sums, spare]), side, lambda r, c: (r, c ^ 2))

    got = got.astype(jnp.float32)
    sums = jnp.split(got[rows:rows + 2 * parts + 2], (parts, 2 * parts, 2 * parts + 1))
    left_got, right_got = unpacked(*sums[:2]).reshape(rows), unpacked(*sums[2:]).reshape(width)
    far_gram = got[:rows] * (jnp.sqrt(left_got) / top)[:, None] * jnp.sqrt(right_got)[None, :]
    return finish(near_gram + far_gram, left_sq + left_got, near_sq + right_got, feat_total)


def on_any_grid(left_docs, right_docs):
    feat_total = left_docs.shape[1] * lax.axis_size("col")
    right_all = lax.all_gather(right_docs, "row", axis=1, tiled=True)
    held = lax.all_to_all(right_all, "col", split_axis=1, concat_axis=0, tiled=True)
    summed = lax.psum_scatter(contract(left_docs, held), "col", scatter_dimension=1, tiled=True)
    left_sq = lax.psum(squares(left_docs), "col")
    right_sq = lax.psum(squares(right_docs), "row")
    return finish(summed, left_sq, right_sq, feat_total)


def solution(mesh):
    square = mesh.shape["row"] == mesh.shape["col"] == 4
    in_specs = (P(("bucket", "row"), "col"), P(("bucket", "col"), "row"))
    out_specs = P(("bucket", "row"), "col")
    return jax.shard_map(
        on_square_grid if square else on_any_grid,
        mesh=mesh, in_specs=in_specs, out_specs=out_specs, check_vma=False,
    )
```

```python
import jax
import jax.numpy as jnp
from jax import lax
from jax.sharding import PartitionSpec as P

epsilon = 1e-06
top = 2.0**15


def contract(left_part, right_part):
    return lax.dot_general(
        left_part, right_part, (((1,), (1,)), ((), ())), preferred_element_type=jnp.float32
    )


def squares(block_part):
    widened = block_part.astype(jnp.float32)
    return jnp.sum(widened * widened, axis=1)


def moved(value, side, place):
    pairs = []
    for row in range(side):
        for col in range(side):
            target = place(row, col)
            if target is not None:
                pairs.append((row * side + col, target[0] * side + target[1]))
    return lax.ppermute(value, ("row", "col"), pairs)


def finish(summed, left_sq, right_sq, feat_total):
    left_scale = lax.rsqrt(left_sq / feat_total + epsilon)
    right_scale = lax.rsqrt(right_sq / feat_total + epsilon)
    return summed / feat_total * left_scale[:, None] * right_scale[None, :]


def packed(sums):
    root = 16.0 * jnp.sqrt(jnp.sqrt(jnp.sqrt(jnp.maximum(sums, 1e-36))))
    high = lax.reduce_precision(root, 5, 10)
    low = lax.reduce_precision((root - high) * 1024.0, 5, 10)
    return high.astype(jnp.float16), low.astype(jnp.float16), unpacked(high, low)


def unpacked(high, low):
    root = (high + low / 1024.0) / 16.0
    for _ in range(3):
        root = root * root
    return root


def on_square_grid(left_docs, right_docs):
    side = lax.axis_size("col")
    feat_total = left_docs.shape[1] * side
    rows, width = left_docs.shape[0], right_docs.shape[0]
    row, col = lax.axis_index("row"), lax.axis_index("col")
    at_home = (row >> 1) == (col >> 1)
    same = (row & 1) == (col & 1)

    def other_core(block):
        return moved(block, side, lambda r, c: (r ^ 1, c))

    def over_x(block):
        return moved(block, side, lambda r, c: (r ^ 2, c))

    def over_middle(block):
        return moved(block, side, lambda r, c: (r, c ^ 2))

    part = width * 3 // 8
    swapped = over_x(right_docs)
    arrived = over_middle(right_docs[:part])
    left_other = moved(left_docs, side, lambda r, c: (r, c ^ 1))
    near, leaving = lax.optimization_barrier(
        (jnp.where(at_home, right_docs, swapped), jnp.where(at_home, swapped[part:], right_docs[part:]))
    )
    arrived, left_other = lax.optimization_barrier((arrived, left_other))
    cross = jnp.concatenate([jnp.where(at_home, arrived, over_x(arrived)), over_middle(leaving)])
    cross = lax.optimization_barrier(cross)
    lefts = lax.optimization_barrier((jnp.where(same, left_docs, left_other), jnp.where(same, left_other, left_docs)))

    def half_sum(mine):
        blocks = (mine, other_core(mine))
        gram = sum(contract(left, right) for left, right in zip(lefts, blocks))
        return gram, sum(squares(block) for block in blocks)

    near_gram, near_sq = half_sum(near)
    cross_gram, cross_sq = half_sum(cross)
    left_sq = squares(left_docs) + squares(left_other)

    left_high, left_low, left_read = packed(left_sq)
    right_high, right_low, right_read = packed(cross_sq)
    tile = cross_gram * (top * lax.rsqrt(left_read))[:, None] * lax.rsqrt(right_read)[None, :]
    parts = rows // width
    sums = [left_high.reshape(parts, width), left_low.reshape(parts, width), right_high[None], right_low[None]]
    spare = jnp.zeros((-(2 * parts + 2) % 8, width), jnp.float16)
    got = moved(jnp.concatenate([tile.astype(jnp.float16), *sums, spare]), side, lambda r, c: (r, c ^ 2))

    got = got.astype(jnp.float32)
    sums = jnp.split(got[rows:rows + 2 * parts + 2], (parts, 2 * parts, 2 * parts + 1))
    left_got, right_got = unpacked(*sums[:2]).reshape(rows), unpacked(*sums[2:]).reshape(width)
    far_gram = got[:rows] * (jnp.sqrt(left_got) / top)[:, None] * jnp.sqrt(right_got)[None, :]
    return finish(near_gram + far_gram, left_sq + left_got, near_sq + right_got, feat_total)


def on_any_grid(left_docs, right_docs):
    feat_total = left_docs.shape[1] * lax.axis_size("col")
    right_all = lax.all_gather(right_docs, "row", axis=1, tiled=True)
    held = lax.all_to_all(right_all, "col", split_axis=1, concat_axis=0, tiled=True)
    summed = lax.psum_scatter(contract(left_docs, held), "col", scatter_dimension=1, tiled=True)
    left_sq = lax.psum(squares(left_docs), "col")
    right_sq = lax.psum(squares(right_docs), "row")
    return finish(summed, left_sq, right_sq, feat_total)


def solution(mesh):
    square = mesh.shape["row"] == mesh.shape["col"] == 4
    in_specs = (P(("bucket", "row"), "col"), P(("bucket", "col"), "row"))
    out_specs = P(("bucket", "row"), "col")
    return jax.shard_map(
        on_square_grid if square else on_any_grid,
        mesh=mesh, in_specs=in_specs, out_specs=out_specs, check_vma=False,
    )
```

```python
import jax
import jax.numpy as jnp
from jax import lax
from jax.sharding import PartitionSpec as P

epsilon = 1e-06
top = 2.0**15


def contract(left_part, right_part):
    return lax.dot_general(
        left_part, right_part, (((1,), (1,)), ((), ())), preferred_element_type=jnp.float32
    )


def squares(block_part):
    widened = block_part.astype(jnp.float32)
    return jnp.sum(widened * widened, axis=1)


def moved(value, side, place):
    pairs = []
    for row in range(side):
        for col in range(side):
            target = place(row, col)
            if target is not None:
                pairs.append((row * side + col, target[0] * side + target[1]))
    return lax.ppermute(value, ("row", "col"), pairs)


def finish(summed, left_sq, right_sq, feat_total):
    left_scale = lax.rsqrt(left_sq / feat_total + epsilon)
    right_scale = lax.rsqrt(right_sq / feat_total + epsilon)
    return summed / feat_total * left_scale[:, None] * right_scale[None, :]


def packed(sums):
    root = 16.0 * jnp.sqrt(jnp.sqrt(jnp.sqrt(jnp.maximum(sums, 1e-36))))
    high = lax.reduce_precision(root, 5, 10)
    low = lax.reduce_precision((root - high) * 1024.0, 5, 10)
    return high.astype(jnp.float16), low.astype(jnp.float16), unpacked(high, low)


def unpacked(high, low):
    root = (high + low / 1024.0) / 16.0
    for _ in range(3):
        root = root * root
    return root


def on_square_grid(left_docs, right_docs):
    side = lax.axis_size("col")
    feat_total = left_docs.shape[1] * side
    rows, width = left_docs.shape[0], right_docs.shape[0]
    row, col = lax.axis_index("row"), lax.axis_index("col")
    at_home = (row >> 1) == (col >> 1)
    same = (row & 1) == (col & 1)

    def other_core(block):
        return moved(block, side, lambda r, c: (r ^ 1, c))

    swapped = moved(right_docs, side, lambda r, c: (r ^ 2, c))
    left_other = moved(left_docs, side, lambda r, c: (r, c ^ 1))
    near, leaving = lax.optimization_barrier(
        (jnp.where(at_home, right_docs, swapped), jnp.split(jnp.where(at_home, swapped, right_docs), 2))
    )
    cross = jnp.concatenate([moved(part, side, lambda r, c: (r, c ^ 2)) for part in leaving])
    cross = lax.optimization_barrier(cross)
    lefts = lax.optimization_barrier((jnp.where(same, left_docs, left_other), jnp.where(same, left_other, left_docs)))

    def half_sum(mine):
        blocks = (mine, other_core(mine))
        gram = sum(contract(left, right) for left, right in zip(lefts, blocks))
        return gram, sum(squares(block) for block in blocks)

    near_gram, near_sq = half_sum(near)
    cross_gram, cross_sq = half_sum(cross)
    left_sq = squares(left_docs) + squares(left_other)

    left_high, left_low, left_read = packed(left_sq)
    right_high, right_low, right_read = packed(cross_sq)
    tile = cross_gram * (top * lax.rsqrt(left_read))[:, None] * lax.rsqrt(right_read)[None, :]
    parts = rows // width
    sums = [left_high.reshape(parts, width), left_low.reshape(parts, width), right_high[None], right_low[None]]
    spare = jnp.zeros((-(2 * parts + 2) % 8, width), jnp.float16)
    got = moved(jnp.concatenate([tile.astype(jnp.float16), *sums, spare]), side, lambda r, c: (r, c ^ 2))

    got = got.astype(jnp.float32)
    sums = jnp.split(got[rows:rows + 2 * parts + 2], (parts, 2 * parts, 2 * parts + 1))
    left_got, right_got = unpacked(*sums[:2]).reshape(rows), unpacked(*sums[2:]).reshape(width)
    far_gram = got[:rows] * (jnp.sqrt(left_got) / top)[:, None] * jnp.sqrt(right_got)[None, :]
    return finish(near_gram + far_gram, left_sq + left_got, near_sq + right_got, feat_total)


def on_any_grid(left_docs, right_docs):
    feat_total = left_docs.shape[1] * lax.axis_size("col")
    right_all = lax.all_gather(right_docs, "row", axis=1, tiled=True)
    held = lax.all_to_all(right_all, "col", split_axis=1, concat_axis=0, tiled=True)
    summed = lax.psum_scatter(contract(left_docs, held), "col", scatter_dimension=1, tiled=True)
    left_sq = lax.psum(squares(left_docs), "col")
    right_sq = lax.psum(squares(right_docs), "row")
    return finish(summed, left_sq, right_sq, feat_total)


def solution(mesh):
    square = mesh.shape["row"] == mesh.shape["col"] == 4
    in_specs = (P(("bucket", "row"), "col"), P(("bucket", "col"), "row"))
    out_specs = P(("bucket", "row"), "col")
    return jax.shard_map(
        on_square_grid if square else on_any_grid,
        mesh=mesh, in_specs=in_specs, out_specs=out_specs, check_vma=False,
    )
```

```python
import jax
import jax.numpy as jnp
from jax import lax
from jax.experimental import pallas as pl
from jax.experimental.pallas import tpu as pltpu
from jax.sharding import PartitionSpec as P

epsilon = 1e-06
top = 2.0**15


def contract(left_part, right_part):
    return lax.dot_general(
        left_part, right_part, (((1,), (1,)), ((), ())), preferred_element_type=jnp.float32
    )


def squares(block_part):
    widened = block_part.astype(jnp.float32)
    return jnp.sum(widened * widened, axis=1)


def moved(value, side, place):
    pairs = []
    for row in range(side):
        for col in range(side):
            target = place(row, col)
            if target is not None:
                pairs.append((row * side + col, target[0] * side + target[1]))
    return lax.ppermute(value, ("row", "col"), pairs)


def finish(summed, left_sq, right_sq, feat_total):
    left_scale = lax.rsqrt(left_sq / feat_total + epsilon)
    right_scale = lax.rsqrt(right_sq / feat_total + epsilon)
    return summed / feat_total * left_scale[:, None] * right_scale[None, :]


def packed(sums):
    root = 16.0 * jnp.sqrt(jnp.sqrt(jnp.sqrt(jnp.maximum(sums, 1e-36))))
    high = lax.reduce_precision(root, 5, 10)
    low = lax.reduce_precision((root - high) * 1024.0, 5, 10)
    return high.astype(jnp.float16), low.astype(jnp.float16), unpacked(high, low)


def unpacked(high, low):
    root = (high + low / 1024.0) / 16.0
    for _ in range(3):
        root = root * root
    return root


def halves_kernel(block, first, second):
    half = first.shape[0]
    first[...] = block[:half]
    second[...] = block[half:]


def halves_of(block):
    half = jax.ShapeDtypeStruct((block.shape[0] // 2, block.shape[1]), block.dtype)
    return pl.pallas_call(
        halves_kernel,
        out_shape=[half, half],
        in_specs=[pl.BlockSpec(memory_space=pltpu.VMEM)],
        out_specs=[pl.BlockSpec(memory_space=pltpu.VMEM)] * 2,
        cost_estimate=pl.CostEstimate(flops=0, bytes_accessed=4 * block.size, transcendentals=0),
    )(block)


def on_square_grid(left_docs, right_docs):
    side = lax.axis_size("col")
    feat_total = left_docs.shape[1] * side
    rows, width = left_docs.shape[0], right_docs.shape[0]
    row, col = lax.axis_index("row"), lax.axis_index("col")
    at_home = (row >> 1) == (col >> 1)
    same = (row & 1) == (col & 1)

    def other_core(block):
        return moved(block, side, lambda r, c: (r ^ 1, c))

    nears, crosses = [], []
    for half in halves_of(right_docs):
        swapped = moved(half, side, lambda r, c: (r ^ 2, c))
        near, leaving = lax.optimization_barrier((jnp.where(at_home, half, swapped), jnp.where(at_home, swapped, half)))
        nears.append(near)
        crosses.append(moved(leaving, side, lambda r, c: (r, c ^ 2)))
    left_other = moved(left_docs, side, lambda r, c: (r, c ^ 1))
    near, cross = lax.optimization_barrier(jnp.concatenate(nears)), lax.optimization_barrier(jnp.concatenate(crosses))
    lefts = lax.optimization_barrier((jnp.where(same, left_docs, left_other), jnp.where(same, left_other, left_docs)))

    def half_sum(mine):
        blocks = (mine, other_core(mine))
        gram = sum(contract(left, right) for left, right in zip(lefts, blocks))
        return gram, sum(squares(block) for block in blocks)

    near_gram, near_sq = half_sum(near)
    cross_gram, cross_sq = half_sum(cross)
    left_sq = squares(left_docs) + squares(left_other)

    left_high, left_low, left_read = packed(left_sq)
    right_high, right_low, right_read = packed(cross_sq)
    tile = cross_gram * (top * lax.rsqrt(left_read))[:, None] * lax.rsqrt(right_read)[None, :]
    parts = rows // width
    sums = [left_high.reshape(parts, width), left_low.reshape(parts, width), right_high[None], right_low[None]]
    spare = jnp.zeros((-(2 * parts + 2) % 8, width), jnp.float16)
    got = moved(jnp.concatenate([tile.astype(jnp.float16), *sums, spare]), side, lambda r, c: (r, c ^ 2))

    got = got.astype(jnp.float32)
    sums = jnp.split(got[rows:rows + 2 * parts + 2], (parts, 2 * parts, 2 * parts + 1))
    left_got, right_got = unpacked(*sums[:2]).reshape(rows), unpacked(*sums[2:]).reshape(width)
    far_gram = got[:rows] * (jnp.sqrt(left_got) / top)[:, None] * jnp.sqrt(right_got)[None, :]
    return finish(near_gram + far_gram, left_sq + left_got, near_sq + right_got, feat_total)


def on_any_grid(left_docs, right_docs):
    feat_total = left_docs.shape[1] * lax.axis_size("col")
    right_all = lax.all_gather(right_docs, "row", axis=1, tiled=True)
    held = lax.all_to_all(right_all, "col", split_axis=1, concat_axis=0, tiled=True)
    summed = lax.psum_scatter(contract(left_docs, held), "col", scatter_dimension=1, tiled=True)
    left_sq = lax.psum(squares(left_docs), "col")
    right_sq = lax.psum(squares(right_docs), "row")
    return finish(summed, left_sq, right_sq, feat_total)


def solution(mesh):
    square = mesh.shape["row"] == mesh.shape["col"] == 4
    in_specs = (P(("bucket", "row"), "col"), P(("bucket", "col"), "row"))
    out_specs = P(("bucket", "row"), "col")
    return jax.shard_map(
        on_square_grid if square else on_any_grid,
        mesh=mesh, in_specs=in_specs, out_specs=out_specs, check_vma=False,
    )
```

```python
import jax
import jax.numpy as jnp
from jax import lax
from jax.sharding import PartitionSpec as P

epsilon = 1e-06
top = 2.0**15


def contract(left_part, right_part):
    return lax.dot_general(
        left_part, right_part, (((1,), (1,)), ((), ())), preferred_element_type=jnp.float32
    )


def squares(block_part):
    widened = block_part.astype(jnp.float32)
    return jnp.sum(widened * widened, axis=1)


def moved(value, side, place):
    pairs = []
    for row in range(side):
        for col in range(side):
            target = place(row, col)
            if target is not None:
                pairs.append((row * side + col, target[0] * side + target[1]))
    return lax.ppermute(value, ("row", "col"), pairs)


def finish(summed, left_sq, right_sq, feat_total):
    left_scale = lax.rsqrt(left_sq / feat_total + epsilon)
    right_scale = lax.rsqrt(right_sq / feat_total + epsilon)
    return summed / feat_total * left_scale[:, None] * right_scale[None, :]


def packed(sums):
    root = 16.0 * jnp.sqrt(jnp.sqrt(jnp.sqrt(jnp.maximum(sums, 1e-36))))
    high = lax.reduce_precision(root, 5, 10)
    low = lax.reduce_precision((root - high) * 1024.0, 5, 10)
    return high.astype(jnp.float16), low.astype(jnp.float16), unpacked(high, low)


def unpacked(high, low):
    root = (high + low / 1024.0) / 16.0
    for _ in range(3):
        root = root * root
    return root


def on_square_grid(left_docs, right_docs):
    side = lax.axis_size("col")
    feat_total = left_docs.shape[1] * side
    rows, width = left_docs.shape[0], right_docs.shape[0]
    row, col = lax.axis_index("row"), lax.axis_index("col")
    at_home = (row >> 1) == (col >> 1)
    same = (row & 1) == (col & 1)

    def other_core(block):
        return moved(block, side, lambda r, c: (r ^ 1, c))

    nears, crosses = [], []
    for half in (right_docs[:width // 2], right_docs[width // 2:]):
        swapped = moved(half, side, lambda r, c: (r ^ 2, c))
        near, leaving = lax.optimization_barrier((jnp.where(at_home, half, swapped), jnp.where(at_home, swapped, half)))
        nears.append(near)
        crosses.append(moved(leaving, side, lambda r, c: (r, c ^ 2)))
    left_other = moved(left_docs, side, lambda r, c: (r, c ^ 1))
    near, cross = lax.optimization_barrier(jnp.concatenate(nears)), lax.optimization_barrier(jnp.concatenate(crosses))
    lefts = lax.optimization_barrier((jnp.where(same, left_docs, left_other), jnp.where(same, left_other, left_docs)))

    def half_sum(mine, other):
        gram = sum(contract(left, right) for left, right in zip(lefts, (mine, other)))
        return gram, squares(mine) + squares(other)

    near_other = other_core(near)
    cross_gram = contract(lefts[0], cross)
    cross_other, cross_gram = lax.optimization_barrier((other_core(cross), cross_gram))
    cross_gram = cross_gram + contract(lefts[1], cross_other)
    cross_sq = squares(cross) + squares(cross_other)
    left_sq = squares(left_docs) + squares(left_other)

    left_high, left_low, left_read = packed(left_sq)
    right_high, right_low, right_read = packed(cross_sq)
    tile = cross_gram * (top * lax.rsqrt(left_read))[:, None] * lax.rsqrt(right_read)[None, :]
    parts = rows // width
    sums = [left_high.reshape(parts, width), left_low.reshape(parts, width), right_high[None], right_low[None]]
    spare = jnp.zeros((-(2 * parts + 2) % 8, width), jnp.float16)
    message = jnp.concatenate([tile.astype(jnp.float16), *sums, spare])
    got = moved(message, side, lambda r, c: (r, c ^ 2))

    near_other, _ = lax.optimization_barrier((near_other, message))
    near_gram, near_sq = half_sum(near, near_other)
    near_gram, got = lax.optimization_barrier((near_gram, got))
    got = got.astype(jnp.float32)
    sums = jnp.split(got[rows:rows + 2 * parts + 2], (parts, 2 * parts, 2 * parts + 1))
    left_got, right_got = unpacked(*sums[:2]).reshape(rows), unpacked(*sums[2:]).reshape(width)
    far_gram = got[:rows] * (jnp.sqrt(left_got) / top)[:, None] * jnp.sqrt(right_got)[None, :]
    return finish(near_gram + far_gram, left_sq + left_got, near_sq + right_got, feat_total)


def on_any_grid(left_docs, right_docs):
    feat_total = left_docs.shape[1] * lax.axis_size("col")
    right_all = lax.all_gather(right_docs, "row", axis=1, tiled=True)
    held = lax.all_to_all(right_all, "col", split_axis=1, concat_axis=0, tiled=True)
    summed = lax.psum_scatter(contract(left_docs, held), "col", scatter_dimension=1, tiled=True)
    left_sq = lax.psum(squares(left_docs), "col")
    right_sq = lax.psum(squares(right_docs), "row")
    return finish(summed, left_sq, right_sq, feat_total)


def solution(mesh):
    square = mesh.shape["row"] == mesh.shape["col"] == 4
    in_specs = (P(("bucket", "row"), "col"), P(("bucket", "col"), "row"))
    out_specs = P(("bucket", "row"), "col")
    return jax.shard_map(
        on_square_grid if square else on_any_grid,
        mesh=mesh, in_specs=in_specs, out_specs=out_specs, check_vma=False,
    )
```

```python
import jax
import jax.numpy as jnp
from jax import lax
from jax.sharding import PartitionSpec as P

epsilon = 1e-06
top = 2.0**15


def contract(left_part, right_part):
    return lax.dot_general(
        left_part, right_part, (((1,), (1,)), ((), ())), preferred_element_type=jnp.float32
    )


def squares(block_part):
    widened = block_part.astype(jnp.float32)
    return jnp.sum(widened * widened, axis=1)


def moved(value, side, place):
    pairs = []
    for row in range(side):
        for col in range(side):
            target = place(row, col)
            if target is not None:
                pairs.append((row * side + col, target[0] * side + target[1]))
    return lax.ppermute(value, ("row", "col"), pairs)


def finish(summed, left_sq, right_sq, feat_total):
    left_scale = lax.rsqrt(left_sq / feat_total + epsilon)
    right_scale = lax.rsqrt(right_sq / feat_total + epsilon)
    return summed / feat_total * left_scale[:, None] * right_scale[None, :]


def packed(sums):
    root = 16.0 * jnp.sqrt(jnp.sqrt(jnp.sqrt(jnp.maximum(sums, 1e-36))))
    high = lax.reduce_precision(root, 5, 10)
    low = lax.reduce_precision((root - high) * 1024.0, 5, 10)
    return high.astype(jnp.float16), low.astype(jnp.float16), unpacked(high, low)


def unpacked(high, low):
    root = (high + low / 1024.0) / 16.0
    for _ in range(3):
        root = root * root
    return root


def on_square_grid(left_docs, right_docs):
    side = lax.axis_size("col")
    feat_total = left_docs.shape[1] * side
    rows, width = left_docs.shape[0], right_docs.shape[0]
    row, col = lax.axis_index("row"), lax.axis_index("col")
    at_home = (row >> 1) == (col >> 1)
    same = (row & 1) == (col & 1)

    def other_core(block):
        return moved(block, side, lambda r, c: (r ^ 1, c))

    nears, crosses = [], []
    for half in (right_docs[:width // 2], right_docs[width // 2:]):
        swapped = moved(half, side, lambda r, c: (r ^ 2, c))
        near, leaving = lax.optimization_barrier((jnp.where(at_home, half, swapped), jnp.where(at_home, swapped, half)))
        nears.append(near)
        crosses.append(moved(leaving, side, lambda r, c: (r, c ^ 2)))
    left_other = moved(left_docs, side, lambda r, c: (r, c ^ 1))
    near, cross = lax.optimization_barrier(jnp.concatenate(nears)), lax.optimization_barrier(jnp.concatenate(crosses))
    lefts = lax.optimization_barrier((jnp.where(same, left_docs, left_other), jnp.where(same, left_other, left_docs)))

    def half_sum(mine, other):
        gram = sum(contract(left, right) for left, right in zip(lefts, (mine, other)))
        return gram, squares(mine) + squares(other)

    near_other = other_core(near)
    cross_gram = contract(lefts[0], cross)
    cross_other, cross_gram = lax.optimization_barrier((jnp.concatenate([other_core(part) for part in crosses]), cross_gram))
    cross_gram = cross_gram + contract(lefts[1], cross_other)
    cross_sq = squares(cross) + squares(cross_other)
    left_sq = squares(left_docs) + squares(left_other)

    left_high, left_low, left_read = packed(left_sq)
    right_high, right_low, right_read = packed(cross_sq)
    tile = cross_gram * (top * lax.rsqrt(left_read))[:, None] * lax.rsqrt(right_read)[None, :]
    parts = rows // width
    sums = [left_high.reshape(parts, width), left_low.reshape(parts, width), right_high[None], right_low[None]]
    spare = jnp.zeros((-(2 * parts + 2) % 8, width), jnp.float16)
    message = jnp.concatenate([tile.astype(jnp.float16), *sums, spare])
    got = moved(message, side, lambda r, c: (r, c ^ 2))

    near_other, _ = lax.optimization_barrier((near_other, message))
    near_gram, near_sq = half_sum(near, near_other)
    near_gram, got = lax.optimization_barrier((near_gram, got))
    got = got.astype(jnp.float32)
    sums = jnp.split(got[rows:rows + 2 * parts + 2], (parts, 2 * parts, 2 * parts + 1))
    left_got, right_got = unpacked(*sums[:2]).reshape(rows), unpacked(*sums[2:]).reshape(width)
    far_gram = got[:rows] * (jnp.sqrt(left_got) / top)[:, None] * jnp.sqrt(right_got)[None, :]
    return finish(near_gram + far_gram, left_sq + left_got, near_sq + right_got, feat_total)


def on_any_grid(left_docs, right_docs):
    feat_total = left_docs.shape[1] * lax.axis_size("col")
    right_all = lax.all_gather(right_docs, "row", axis=1, tiled=True)
    held = lax.all_to_all(right_all, "col", split_axis=1, concat_axis=0, tiled=True)
    summed = lax.psum_scatter(contract(left_docs, held), "col", scatter_dimension=1, tiled=True)
    left_sq = lax.psum(squares(left_docs), "col")
    right_sq = lax.psum(squares(right_docs), "row")
    return finish(summed, left_sq, right_sq, feat_total)


def solution(mesh):
    square = mesh.shape["row"] == mesh.shape["col"] == 4
    in_specs = (P(("bucket", "row"), "col"), P(("bucket", "col"), "row"))
    out_specs = P(("bucket", "row"), "col")
    return jax.shard_map(
        on_square_grid if square else on_any_grid,
        mesh=mesh, in_specs=in_specs, out_specs=out_specs, check_vma=False,
    )
```

```python
import jax
import jax.numpy as jnp
from jax import lax
from jax.sharding import PartitionSpec as P

epsilon = 1e-06
top = 2.0**15


def contract(left_part, right_part):
    return lax.dot_general(
        left_part, right_part, (((1,), (1,)), ((), ())), preferred_element_type=jnp.float32
    )


def squares(block_part):
    widened = block_part.astype(jnp.float32)
    return jnp.sum(widened * widened, axis=1)


def moved(value, side, place):
    pairs = []
    for row in range(side):
        for col in range(side):
            target = place(row, col)
            if target is not None:
                pairs.append((row * side + col, target[0] * side + target[1]))
    return lax.ppermute(value, ("row", "col"), pairs)


def finish(summed, left_sq, right_sq, feat_total):
    left_scale = lax.rsqrt(left_sq / feat_total + epsilon)
    right_scale = lax.rsqrt(right_sq / feat_total + epsilon)
    return summed / feat_total * left_scale[:, None] * right_scale[None, :]


def packed(sums):
    root = 16.0 * jnp.sqrt(jnp.sqrt(jnp.sqrt(jnp.maximum(sums, 1e-36))))
    high = lax.reduce_precision(root, 5, 10)
    low = lax.reduce_precision((root - high) * 1024.0, 5, 10)
    return high.astype(jnp.float16), low.astype(jnp.float16), unpacked(high, low)


def unpacked(high, low):
    root = (high + low / 1024.0) / 16.0
    for _ in range(3):
        root = root * root
    return root


def on_square_grid(left_docs, right_docs):
    side = lax.axis_size("col")
    feat_total = left_docs.shape[1] * side
    rows, width = left_docs.shape[0], right_docs.shape[0]
    row, col = lax.axis_index("row"), lax.axis_index("col")
    at_home = (row >> 1) == (col >> 1)
    same = (row & 1) == (col & 1)

    def other_core(block):
        return moved(block, side, lambda r, c: (r ^ 1, c))

    nears, crosses = [], []
    for half in lax.optimization_barrier((right_docs[:width // 2], right_docs[width // 2:])):
        swapped = moved(half, side, lambda r, c: (r ^ 2, c))
        near, leaving = lax.optimization_barrier((jnp.where(at_home, half, swapped), jnp.where(at_home, swapped, half)))
        nears.append(near)
        crosses.append(moved(leaving, side, lambda r, c: (r, c ^ 2)))
    left_other = moved(left_docs, side, lambda r, c: (r, c ^ 1))
    near, cross = lax.optimization_barrier(jnp.concatenate(nears)), lax.optimization_barrier(jnp.concatenate(crosses))
    lefts = lax.optimization_barrier((jnp.where(same, left_docs, left_other), jnp.where(same, left_other, left_docs)))

    def half_sum(mine, other):
        gram = sum(contract(left, right) for left, right in zip(lefts, (mine, other)))
        return gram, squares(mine) + squares(other)

    near_other = other_core(near)
    cross_gram = contract(lefts[0], cross)
    cross_other, cross_gram = lax.optimization_barrier((jnp.concatenate([other_core(part) for part in crosses]), cross_gram))
    cross_gram = cross_gram + contract(lefts[1], cross_other)
    cross_sq = squares(cross) + squares(cross_other)
    left_sq = squares(left_docs) + squares(left_other)

    left_high, left_low, left_read = packed(left_sq)
    right_high, right_low, right_read = packed(cross_sq)
    tile = cross_gram * (top * lax.rsqrt(left_read))[:, None] * lax.rsqrt(right_read)[None, :]
    parts = rows // width
    sums = [left_high.reshape(parts, width), left_low.reshape(parts, width), right_high[None], right_low[None]]
    spare = jnp.zeros((-(2 * parts + 2) % 8, width), jnp.float16)
    message = jnp.concatenate([tile.astype(jnp.float16), *sums, spare])
    got = moved(message, side, lambda r, c: (r, c ^ 2))

    near_other, _ = lax.optimization_barrier((near_other, message))
    near_gram, near_sq = half_sum(near, near_other)
    near_gram, got = lax.optimization_barrier((near_gram, got))
    got = got.astype(jnp.float32)
    sums = jnp.split(got[rows:rows + 2 * parts + 2], (parts, 2 * parts, 2 * parts + 1))
    left_got, right_got = unpacked(*sums[:2]).reshape(rows), unpacked(*sums[2:]).reshape(width)
    far_gram = got[:rows] * (jnp.sqrt(left_got) / top)[:, None] * jnp.sqrt(right_got)[None, :]
    return finish(near_gram + far_gram, left_sq + left_got, near_sq + right_got, feat_total)


def on_any_grid(left_docs, right_docs):
    feat_total = left_docs.shape[1] * lax.axis_size("col")
    right_all = lax.all_gather(right_docs, "row", axis=1, tiled=True)
    held = lax.all_to_all(right_all, "col", split_axis=1, concat_axis=0, tiled=True)
    summed = lax.psum_scatter(contract(left_docs, held), "col", scatter_dimension=1, tiled=True)
    left_sq = lax.psum(squares(left_docs), "col")
    right_sq = lax.psum(squares(right_docs), "row")
    return finish(summed, left_sq, right_sq, feat_total)


def solution(mesh):
    square = mesh.shape["row"] == mesh.shape["col"] == 4
    in_specs = (P(("bucket", "row"), "col"), P(("bucket", "col"), "row"))
    out_specs = P(("bucket", "row"), "col")
    return jax.shard_map(
        on_square_grid if square else on_any_grid,
        mesh=mesh, in_specs=in_specs, out_specs=out_specs, check_vma=False,
    )
```

```python
import jax
import jax.numpy as jnp
from jax import lax
from jax.sharding import PartitionSpec as P

epsilon = 1e-06
top = 2.0**15


def contract(left_part, right_part):
    return lax.dot_general(
        left_part, right_part, (((1,), (1,)), ((), ())), preferred_element_type=jnp.float32
    )


def squares(block_part):
    widened = block_part.astype(jnp.float32)
    return jnp.sum(widened * widened, axis=1)


def moved(value, side, place):
    pairs = []
    for row in range(side):
        for col in range(side):
            target = place(row, col)
            if target is not None:
                pairs.append((row * side + col, target[0] * side + target[1]))
    return lax.ppermute(value, ("row", "col"), pairs)


def finish(summed, left_sq, right_sq, feat_total):
    left_scale = lax.rsqrt(left_sq / feat_total + epsilon)
    right_scale = lax.rsqrt(right_sq / feat_total + epsilon)
    return summed / feat_total * left_scale[:, None] * right_scale[None, :]


def packed(sums):
    root = 16.0 * jnp.sqrt(jnp.sqrt(jnp.sqrt(jnp.maximum(sums, 1e-36))))
    high = lax.reduce_precision(root, 5, 10)
    low = lax.reduce_precision((root - high) * 1024.0, 5, 10)
    return high.astype(jnp.float16), low.astype(jnp.float16), unpacked(high, low)


def unpacked(high, low):
    root = (high + low / 1024.0) / 16.0
    for _ in range(3):
        root = root * root
    return root


def on_square_grid(left_docs, right_docs):
    side = lax.axis_size("col")
    feat_total = left_docs.shape[1] * side
    rows, width = left_docs.shape[0], right_docs.shape[0]
    row, col = lax.axis_index("row"), lax.axis_index("col")
    at_home = (row >> 1) == (col >> 1)
    same = (row & 1) == (col & 1)

    def other_core(block):
        return moved(block, side, lambda r, c: (r ^ 1, c))

    nears, crosses = [], []
    for half in lax.optimization_barrier((right_docs[:width // 2], right_docs[width // 2:])):
        swapped = moved(half, side, lambda r, c: (r ^ 2, c))
        near, leaving = lax.optimization_barrier((jnp.where(at_home, half, swapped), jnp.where(at_home, swapped, half)))
        nears.append(near)
        crosses.append(moved(leaving, side, lambda r, c: (r, c ^ 2)))
    left_other = moved(left_docs, side, lambda r, c: (r, c ^ 1))
    near = lax.optimization_barrier(jnp.concatenate(nears))
    near_other = other_core(near)
    crosses[1], near_other = lax.optimization_barrier((crosses[1], near_other))
    cross = lax.optimization_barrier(jnp.concatenate(crosses))
    lefts = lax.optimization_barrier((jnp.where(same, left_docs, left_other), jnp.where(same, left_other, left_docs)))

    def half_sum(mine, other):
        gram = sum(contract(left, right) for left, right in zip(lefts, (mine, other)))
        return gram, squares(mine) + squares(other)

    cross_gram = contract(lefts[0], cross)
    cross_other, cross_gram = lax.optimization_barrier((jnp.concatenate([other_core(part) for part in crosses]), cross_gram))
    cross_gram = cross_gram + contract(lefts[1], cross_other)
    cross_sq = squares(cross) + squares(cross_other)
    left_sq = squares(left_docs) + squares(left_other)

    left_high, left_low, left_read = packed(left_sq)
    right_high, right_low, right_read = packed(cross_sq)
    tile = cross_gram * (top * lax.rsqrt(left_read))[:, None] * lax.rsqrt(right_read)[None, :]
    parts = rows // width
    sums = [left_high.reshape(parts, width), left_low.reshape(parts, width), right_high[None], right_low[None]]
    spare = jnp.zeros((-(2 * parts + 2) % 8, width), jnp.float16)
    message = jnp.concatenate([tile.astype(jnp.float16), *sums, spare])
    got = moved(message, side, lambda r, c: (r, c ^ 2))

    near_other, _ = lax.optimization_barrier((near_other, message))
    near_gram, near_sq = half_sum(near, near_other)
    near_gram, got = lax.optimization_barrier((near_gram, got))
    got = got.astype(jnp.float32)
    sums = jnp.split(got[rows:rows + 2 * parts + 2], (parts, 2 * parts, 2 * parts + 1))
    left_got, right_got = unpacked(*sums[:2]).reshape(rows), unpacked(*sums[2:]).reshape(width)
    far_gram = got[:rows] * (jnp.sqrt(left_got) / top)[:, None] * jnp.sqrt(right_got)[None, :]
    return finish(near_gram + far_gram, left_sq + left_got, near_sq + right_got, feat_total)


def on_any_grid(left_docs, right_docs):
    feat_total = left_docs.shape[1] * lax.axis_size("col")
    right_all = lax.all_gather(right_docs, "row", axis=1, tiled=True)
    held = lax.all_to_all(right_all, "col", split_axis=1, concat_axis=0, tiled=True)
    summed = lax.psum_scatter(contract(left_docs, held), "col", scatter_dimension=1, tiled=True)
    left_sq = lax.psum(squares(left_docs), "col")
    right_sq = lax.psum(squares(right_docs), "row")
    return finish(summed, left_sq, right_sq, feat_total)


def solution(mesh):
    square = mesh.shape["row"] == mesh.shape["col"] == 4
    in_specs = (P(("bucket", "row"), "col"), P(("bucket", "col"), "row"))
    out_specs = P(("bucket", "row"), "col")
    return jax.shard_map(
        on_square_grid if square else on_any_grid,
        mesh=mesh, in_specs=in_specs, out_specs=out_specs, check_vma=False,
    )
```

```python
import jax
import jax.numpy as jnp
from jax import lax
from jax.sharding import PartitionSpec as P

epsilon = 1e-06
top = 2.0**15


def contract(left_part, right_part):
    return lax.dot_general(
        left_part, right_part, (((1,), (1,)), ((), ())), preferred_element_type=jnp.float32
    )


def squares(block_part):
    widened = block_part.astype(jnp.float32)
    return jnp.sum(widened * widened, axis=1)


def moved(value, side, place):
    pairs = []
    for row in range(side):
        for col in range(side):
            target = place(row, col)
            if target is not None:
                pairs.append((row * side + col, target[0] * side + target[1]))
    return lax.ppermute(value, ("row", "col"), pairs)


def finish(summed, left_sq, right_sq, feat_total):
    left_scale = lax.rsqrt(left_sq / feat_total + epsilon)
    right_scale = lax.rsqrt(right_sq / feat_total + epsilon)
    return summed / feat_total * left_scale[:, None] * right_scale[None, :]


def packed(sums):
    root = 16.0 * jnp.sqrt(jnp.sqrt(jnp.sqrt(jnp.maximum(sums, 1e-36))))
    high = lax.reduce_precision(root, 5, 10)
    low = lax.reduce_precision((root - high) * 1024.0, 5, 10)
    return high.astype(jnp.float16), low.astype(jnp.float16), unpacked(high, low)


def unpacked(high, low):
    root = (high + low / 1024.0) / 16.0
    for _ in range(3):
        root = root * root
    return root


def on_square_grid(left_docs, right_docs):
    side = lax.axis_size("col")
    feat_total = left_docs.shape[1] * side
    rows, width = left_docs.shape[0], right_docs.shape[0]
    row, col = lax.axis_index("row"), lax.axis_index("col")
    at_home = (row >> 1) == (col >> 1)
    same = (row & 1) == (col & 1)

    def other_core(block):
        return moved(block, side, lambda r, c: (r ^ 1, c))

    nears, crosses = [], []
    for half in lax.optimization_barrier((right_docs[:width // 2], right_docs[width // 2:])):
        swapped = moved(half, side, lambda r, c: (r ^ 2, c))
        near, leaving = lax.optimization_barrier((jnp.where(at_home, half, swapped), jnp.where(at_home, swapped, half)))
        nears.append(near)
        crosses.append(moved(leaving, side, lambda r, c: (r, c ^ 2)))
    left_other = moved(left_docs, side, lambda r, c: (r, c ^ 1))
    near = lax.optimization_barrier(jnp.concatenate(nears))
    crosses[1], left_other = lax.optimization_barrier((crosses[1], left_other))
    cross = lax.optimization_barrier(jnp.concatenate(crosses))
    lefts = lax.optimization_barrier((jnp.where(same, left_docs, left_other), jnp.where(same, left_other, left_docs)))

    def half_sum(mine, other):
        gram = sum(contract(left, right) for left, right in zip(lefts, (mine, other)))
        return gram, squares(mine) + squares(other)

    near_other = other_core(near)
    cross_gram = contract(lefts[0], cross)
    cross_other, cross_gram = lax.optimization_barrier((other_core(cross), cross_gram))
    cross_gram = cross_gram + contract(lefts[1], cross_other)
    cross_sq = squares(cross) + squares(cross_other)
    left_sq = squares(left_docs) + squares(left_other)

    left_high, left_low, left_read = packed(left_sq)
    right_high, right_low, right_read = packed(cross_sq)
    tile = cross_gram * (top * lax.rsqrt(left_read))[:, None] * lax.rsqrt(right_read)[None, :]
    parts = rows // width
    sums = [left_high.reshape(parts, width), left_low.reshape(parts, width), right_high[None], right_low[None]]
    spare = jnp.zeros((-(2 * parts + 2) % 8, width), jnp.float16)
    message = jnp.concatenate([tile.astype(jnp.float16), *sums, spare])
    got = moved(message, side, lambda r, c: (r, c ^ 2))

    near_other, _ = lax.optimization_barrier((near_other, message))
    near_gram, near_sq = half_sum(near, near_other)
    near_gram, got = lax.optimization_barrier((near_gram, got))
    got = got.astype(jnp.float32)
    sums = jnp.split(got[rows:rows + 2 * parts + 2], (parts, 2 * parts, 2 * parts + 1))
    left_got, right_got = unpacked(*sums[:2]).reshape(rows), unpacked(*sums[2:]).reshape(width)
    far_gram = got[:rows] * (jnp.sqrt(left_got) / top)[:, None] * jnp.sqrt(right_got)[None, :]
    return finish(near_gram + far_gram, left_sq + left_got, near_sq + right_got, feat_total)


def on_any_grid(left_docs, right_docs):
    feat_total = left_docs.shape[1] * lax.axis_size("col")
    right_all = lax.all_gather(right_docs, "row", axis=1, tiled=True)
    held = lax.all_to_all(right_all, "col", split_axis=1, concat_axis=0, tiled=True)
    summed = lax.psum_scatter(contract(left_docs, held), "col", scatter_dimension=1, tiled=True)
    left_sq = lax.psum(squares(left_docs), "col")
    right_sq = lax.psum(squares(right_docs), "row")
    return finish(summed, left_sq, right_sq, feat_total)


def solution(mesh):
    square = mesh.shape["row"] == mesh.shape["col"] == 4
    in_specs = (P(("bucket", "row"), "col"), P(("bucket", "col"), "row"))
    out_specs = P(("bucket", "row"), "col")
    return jax.shard_map(
        on_square_grid if square else on_any_grid,
        mesh=mesh, in_specs=in_specs, out_specs=out_specs, check_vma=False,
    )
```

```python
import jax
import jax.numpy as jnp
from jax import lax
from jax.sharding import PartitionSpec as P

epsilon = 1e-06
top = 2.0**15


def contract(left_part, right_part):
    return lax.dot_general(
        left_part, right_part, (((1,), (1,)), ((), ())), preferred_element_type=jnp.float32
    )


def squares(block_part):
    widened = block_part.astype(jnp.float32)
    return jnp.sum(widened * widened, axis=1)


def moved(value, side, place):
    pairs = []
    for row in range(side):
        for col in range(side):
            target = place(row, col)
            if target is not None:
                pairs.append((row * side + col, target[0] * side + target[1]))
    return lax.ppermute(value, ("row", "col"), pairs)


def finish(summed, left_sq, right_sq, feat_total):
    left_scale = lax.rsqrt(left_sq / feat_total + epsilon)
    right_scale = lax.rsqrt(right_sq / feat_total + epsilon)
    return summed / feat_total * left_scale[:, None] * right_scale[None, :]


def packed(sums):
    root = 16.0 * jnp.sqrt(jnp.sqrt(jnp.sqrt(jnp.maximum(sums, 1e-36))))
    high = lax.reduce_precision(root, 5, 10)
    low = lax.reduce_precision((root - high) * 1024.0, 5, 10)
    return high.astype(jnp.float16), low.astype(jnp.float16), unpacked(high, low)


def unpacked(high, low):
    root = (high + low / 1024.0) / 16.0
    for _ in range(3):
        root = root * root
    return root


def on_square_grid(left_docs, right_docs):
    side = lax.axis_size("col")
    feat_total = left_docs.shape[1] * side
    rows, width = left_docs.shape[0], right_docs.shape[0]
    row, col = lax.axis_index("row"), lax.axis_index("col")
    at_home = (row >> 1) == (col >> 1)
    same = (row & 1) == (col & 1)

    def other_core(block):
        return moved(block, side, lambda r, c: (r ^ 1, c))

    nears, crosses = [], []
    for half in lax.optimization_barrier((right_docs[:width // 2], right_docs[width // 2:])):
        swapped = moved(half, side, lambda r, c: (r ^ 2, c))
        near, leaving = lax.optimization_barrier((jnp.where(at_home, half, swapped), jnp.where(at_home, swapped, half)))
        nears.append(near)
        crosses.append(moved(leaving, side, lambda r, c: (r, c ^ 2)))
    left_other = moved(left_docs, side, lambda r, c: (r, c ^ 1))
    near = lax.optimization_barrier(jnp.concatenate(nears))
    near, left_other = lax.optimization_barrier((near, left_other))
    near_other = other_core(near)
    crosses[1], near_other = lax.optimization_barrier((crosses[1], near_other))
    cross = lax.optimization_barrier(jnp.concatenate(crosses))
    lefts = lax.optimization_barrier((jnp.where(same, left_docs, left_other), jnp.where(same, left_other, left_docs)))

    def half_sum(mine, other):
        gram = sum(contract(left, right) for left, right in zip(lefts, (mine, other)))
        return gram, squares(mine) + squares(other)

    cross_gram = contract(lefts[0], cross)
    cross_other, cross_gram = lax.optimization_barrier((jnp.concatenate([other_core(part) for part in crosses]), cross_gram))
    cross_gram = cross_gram + contract(lefts[1], cross_other)
    cross_sq = squares(cross) + squares(cross_other)
    left_sq = squares(left_docs) + squares(left_other)

    left_high, left_low, left_read = packed(left_sq)
    right_high, right_low, right_read = packed(cross_sq)
    tile = cross_gram * (top * lax.rsqrt(left_read))[:, None] * lax.rsqrt(right_read)[None, :]
    parts = rows // width
    sums = [left_high.reshape(parts, width), left_low.reshape(parts, width), right_high[None], right_low[None]]
    spare = jnp.zeros((-(2 * parts + 2) % 8, width), jnp.float16)
    message = jnp.concatenate([tile.astype(jnp.float16), *sums, spare])
    got = moved(message, side, lambda r, c: (r, c ^ 2))

    near_other, _ = lax.optimization_barrier((near_other, message))
    near_gram, near_sq = half_sum(near, near_other)
    near_gram, got = lax.optimization_barrier((near_gram, got))
    got = got.astype(jnp.float32)
    sums = jnp.split(got[rows:rows + 2 * parts + 2], (parts, 2 * parts, 2 * parts + 1))
    left_got, right_got = unpacked(*sums[:2]).reshape(rows), unpacked(*sums[2:]).reshape(width)
    far_gram = got[:rows] * (jnp.sqrt(left_got) / top)[:, None] * jnp.sqrt(right_got)[None, :]
    return finish(near_gram + far_gram, left_sq + left_got, near_sq + right_got, feat_total)


def on_any_grid(left_docs, right_docs):
    feat_total = left_docs.shape[1] * lax.axis_size("col")
    right_all = lax.all_gather(right_docs, "row", axis=1, tiled=True)
    held = lax.all_to_all(right_all, "col", split_axis=1, concat_axis=0, tiled=True)
    summed = lax.psum_scatter(contract(left_docs, held), "col", scatter_dimension=1, tiled=True)
    left_sq = lax.psum(squares(left_docs), "col")
    right_sq = lax.psum(squares(right_docs), "row")
    return finish(summed, left_sq, right_sq, feat_total)


def solution(mesh):
    square = mesh.shape["row"] == mesh.shape["col"] == 4
    in_specs = (P(("bucket", "row"), "col"), P(("bucket", "col"), "row"))
    out_specs = P(("bucket", "row"), "col")
    return jax.shard_map(
        on_square_grid if square else on_any_grid,
        mesh=mesh, in_specs=in_specs, out_specs=out_specs, check_vma=False,
    )
```

```python
import jax
import jax.numpy as jnp
from jax import lax
from jax.sharding import PartitionSpec as P

epsilon = 1e-06
top = 2.0**15


def contract(left_part, right_part):
    return lax.dot_general(
        left_part, right_part, (((1,), (1,)), ((), ())), preferred_element_type=jnp.float32
    )


def squares(block_part):
    widened = block_part.astype(jnp.float32)
    return jnp.sum(widened * widened, axis=1)


def moved(value, side, place):
    pairs = []
    for row in range(side):
        for col in range(side):
            target = place(row, col)
            if target is not None:
                pairs.append((row * side + col, target[0] * side + target[1]))
    return lax.ppermute(value, ("row", "col"), pairs)


def finish(summed, left_sq, right_sq, feat_total):
    left_scale = lax.rsqrt(left_sq / feat_total + epsilon)
    right_scale = lax.rsqrt(right_sq / feat_total + epsilon)
    return summed / feat_total * left_scale[:, None] * right_scale[None, :]


def packed(sums):
    root = 16.0 * jnp.sqrt(jnp.sqrt(jnp.sqrt(jnp.maximum(sums, 1e-36))))
    high = lax.reduce_precision(root, 5, 10)
    low = lax.reduce_precision((root - high) * 1024.0, 5, 10)
    return high.astype(jnp.float16), low.astype(jnp.float16), unpacked(high, low)


def unpacked(high, low):
    root = (high + low / 1024.0) / 16.0
    for _ in range(3):
        root = root * root
    return root


def on_square_grid(left_docs, right_docs):
    side = lax.axis_size("col")
    feat_total = left_docs.shape[1] * side
    rows, width = left_docs.shape[0], right_docs.shape[0]
    row, col = lax.axis_index("row"), lax.axis_index("col")
    at_home = (row >> 1) == (col >> 1)
    same = (row & 1) == (col & 1)

    def other_core(block):
        return moved(block, side, lambda r, c: (r ^ 1, c))

    nears, crosses = [], []
    for half in lax.optimization_barrier((right_docs[:width // 2], right_docs[width // 2:])):
        swapped = moved(half, side, lambda r, c: (r ^ 2, c))
        near, leaving = lax.optimization_barrier((jnp.where(at_home, half, swapped), jnp.where(at_home, swapped, half)))
        nears.append(near)
        crosses.append(moved(leaving, side, lambda r, c: (r, c ^ 3)))
    left_other = moved(left_docs, side, lambda r, c: (r, c ^ 1))
    near = lax.optimization_barrier(jnp.concatenate(nears))
    near_other = other_core(near)
    crosses[1], near_other = lax.optimization_barrier((crosses[1], near_other))
    cross = lax.optimization_barrier(jnp.concatenate(crosses))
    lefts = lax.optimization_barrier((jnp.where(same, left_docs, left_other), jnp.where(same, left_other, left_docs)))

    def half_sum(mine, other):
        gram = sum(contract(left, right) for left, right in zip(lefts, (mine, other)))
        return gram, squares(mine) + squares(other)

    cross_gram = contract(lefts[0], cross)
    cross_other, cross_gram = lax.optimization_barrier((jnp.concatenate([other_core(part) for part in crosses]), cross_gram))
    cross_gram = cross_gram + contract(lefts[1], cross_other)
    cross_sq = squares(cross) + squares(cross_other)
    left_sq = squares(left_docs) + squares(left_other)

    left_high, left_low, left_read = packed(left_sq)
    right_high, right_low, right_read = packed(cross_sq)
    tile = cross_gram * (top * lax.rsqrt(left_read))[:, None] * lax.rsqrt(right_read)[None, :]
    parts = rows // width
    sums = [left_high.reshape(parts, width), left_low.reshape(parts, width), right_high[None], right_low[None]]
    spare = jnp.zeros((-(2 * parts + 2) % 8, width), jnp.float16)
    message = jnp.concatenate([tile.astype(jnp.float16), *sums, spare])
    got = moved(message, side, lambda r, c: (r, c ^ 3))

    near_other, _ = lax.optimization_barrier((near_other, message))
    near_gram, near_sq = half_sum(near, near_other)
    near_gram, got = lax.optimization_barrier((near_gram, got))
    got = got.astype(jnp.float32)
    sums = jnp.split(got[rows:rows + 2 * parts + 2], (parts, 2 * parts, 2 * parts + 1))
    left_got, right_got = unpacked(*sums[:2]).reshape(rows), unpacked(*sums[2:]).reshape(width)
    far_gram = got[:rows] * (jnp.sqrt(left_got) / top)[:, None] * jnp.sqrt(right_got)[None, :]
    return finish(near_gram + far_gram, left_sq + left_got, near_sq + right_got, feat_total)


def on_any_grid(left_docs, right_docs):
    feat_total = left_docs.shape[1] * lax.axis_size("col")
    right_all = lax.all_gather(right_docs, "row", axis=1, tiled=True)
    held = lax.all_to_all(right_all, "col", split_axis=1, concat_axis=0, tiled=True)
    summed = lax.psum_scatter(contract(left_docs, held), "col", scatter_dimension=1, tiled=True)
    left_sq = lax.psum(squares(left_docs), "col")
    right_sq = lax.psum(squares(right_docs), "row")
    return finish(summed, left_sq, right_sq, feat_total)


def solution(mesh):
    square = mesh.shape["row"] == mesh.shape["col"] == 4
    in_specs = (P(("bucket", "row"), "col"), P(("bucket", "col"), "row"))
    out_specs = P(("bucket", "row"), "col")
    return jax.shard_map(
        on_square_grid if square else on_any_grid,
        mesh=mesh, in_specs=in_specs, out_specs=out_specs, check_vma=False,
    )
```

```python
import jax
import jax.numpy as jnp
from jax import lax
from jax.sharding import PartitionSpec as P

epsilon = 1e-06
top = 2.0**15


def contract(left_part, right_part):
    return lax.dot_general(
        left_part, right_part, (((1,), (1,)), ((), ())), preferred_element_type=jnp.float32
    )


def squares(block_part):
    widened = block_part.astype(jnp.float32)
    return jnp.sum(widened * widened, axis=1)


def moved(value, side, place):
    pairs = []
    for row in range(side):
        for col in range(side):
            target = place(row, col)
            if target is not None:
                pairs.append((row * side + col, target[0] * side + target[1]))
    return lax.ppermute(value, ("row", "col"), pairs)


def finish(summed, left_sq, right_sq, feat_total):
    left_scale = lax.rsqrt(left_sq / feat_total + epsilon)
    right_scale = lax.rsqrt(right_sq / feat_total + epsilon)
    return summed / feat_total * left_scale[:, None] * right_scale[None, :]


def packed(sums):
    root = 16.0 * jnp.sqrt(jnp.sqrt(jnp.sqrt(jnp.maximum(sums, 1e-36))))
    high = lax.reduce_precision(root, 5, 10)
    low = lax.reduce_precision((root - high) * 1024.0, 5, 10)
    return high.astype(jnp.float16), low.astype(jnp.float16), unpacked(high, low)


def unpacked(high, low):
    root = (high + low / 1024.0) / 16.0
    for _ in range(3):
        root = root * root
    return root


def on_square_grid(left_docs, right_docs):
    side = lax.axis_size("col")
    feat_total = left_docs.shape[1] * side
    rows, width = left_docs.shape[0], right_docs.shape[0]
    row, col = lax.axis_index("row"), lax.axis_index("col")
    at_home = (row >> 1) == (col >> 1)
    same = (row & 1) == (col & 1)

    def other_core(block):
        return moved(block, side, lambda r, c: (r ^ 1, c))

    swapped = moved(right_docs, side, lambda r, c: (r ^ 2, c))
    own_sq = squares(left_docs)
    swapped, own_sq = lax.optimization_barrier((swapped, own_sq))
    near, *leaving = lax.optimization_barrier(
        (jnp.where(at_home, right_docs, swapped), *jnp.split(jnp.where(at_home, swapped, right_docs), 2))
    )
    crosses = [moved(part, side, lambda r, c: (r, c ^ 2)) for part in leaving]
    left_other = moved(left_docs, side, lambda r, c: (r, c ^ 1))
    near_other = other_core(near)
    crosses[1], near_other = lax.optimization_barrier((crosses[1], near_other))
    cross = lax.optimization_barrier(jnp.concatenate(crosses))
    lefts = lax.optimization_barrier((jnp.where(same, left_docs, left_other), jnp.where(same, left_other, left_docs)))

    def half_sum(mine, other):
        gram = sum(contract(left, right) for left, right in zip(lefts, (mine, other)))
        return gram, squares(mine) + squares(other)

    cross_gram = contract(lefts[0], cross)
    cross_other, cross_gram = lax.optimization_barrier((jnp.concatenate([other_core(part) for part in crosses]), cross_gram))
    cross_gram = cross_gram + contract(lefts[1], cross_other)
    cross_sq = squares(cross) + squares(cross_other)
    left_sq = own_sq + squares(left_other)

    left_high, left_low, left_read = packed(left_sq)
    right_high, right_low, right_read = packed(cross_sq)
    tile = cross_gram * (top * lax.rsqrt(left_read))[:, None] * lax.rsqrt(right_read)[None, :]
    parts = rows // width
    sums = [left_high.reshape(parts, width), left_low.reshape(parts, width), right_high[None], right_low[None]]
    spare = jnp.zeros((-(2 * parts + 2) % 8, width), jnp.float16)
    message = jnp.concatenate([tile.astype(jnp.float16), *sums, spare])
    got = moved(message, side, lambda r, c: (r, c ^ 2))

    near_other, _ = lax.optimization_barrier((near_other, message))
    near_gram, near_sq = half_sum(near, near_other)
    near_gram, got = lax.optimization_barrier((near_gram, got))
    got = got.astype(jnp.float32)
    sums = jnp.split(got[rows:rows + 2 * parts + 2], (parts, 2 * parts, 2 * parts + 1))
    left_got, right_got = unpacked(*sums[:2]).reshape(rows), unpacked(*sums[2:]).reshape(width)
    far_gram = got[:rows] * (jnp.sqrt(left_got) / top)[:, None] * jnp.sqrt(right_got)[None, :]
    return finish(near_gram + far_gram, left_sq + left_got, near_sq + right_got, feat_total)


def on_any_grid(left_docs, right_docs):
    feat_total = left_docs.shape[1] * lax.axis_size("col")
    right_all = lax.all_gather(right_docs, "row", axis=1, tiled=True)
    held = lax.all_to_all(right_all, "col", split_axis=1, concat_axis=0, tiled=True)
    summed = lax.psum_scatter(contract(left_docs, held), "col", scatter_dimension=1, tiled=True)
    left_sq = lax.psum(squares(left_docs), "col")
    right_sq = lax.psum(squares(right_docs), "row")
    return finish(summed, left_sq, right_sq, feat_total)


def solution(mesh):
    square = mesh.shape["row"] == mesh.shape["col"] == 4
    in_specs = (P(("bucket", "row"), "col"), P(("bucket", "col"), "row"))
    out_specs = P(("bucket", "row"), "col")
    return jax.shard_map(
        on_square_grid if square else on_any_grid,
        mesh=mesh, in_specs=in_specs, out_specs=out_specs, check_vma=False,
    )
```

```python
import jax
import jax.numpy as jnp
from jax import lax
from jax.sharding import PartitionSpec as P

epsilon = 1e-06
top = 2.0**15


def contract(left_part, right_part):
    return lax.dot_general(
        left_part, right_part, (((1,), (1,)), ((), ())), preferred_element_type=jnp.float32
    )


def squares(block_part):
    widened = block_part.astype(jnp.float32)
    return jnp.sum(widened * widened, axis=1)


def moved(value, side, place):
    pairs = []
    for row in range(side):
        for col in range(side):
            target = place(row, col)
            if target is not None:
                pairs.append((row * side + col, target[0] * side + target[1]))
    return lax.ppermute(value, ("row", "col"), pairs)


def finish(summed, left_sq, right_sq, feat_total):
    left_scale = lax.rsqrt(left_sq / feat_total + epsilon)
    right_scale = lax.rsqrt(right_sq / feat_total + epsilon)
    return summed / feat_total * left_scale[:, None] * right_scale[None, :]


def packed(sums):
    root = 16.0 * jnp.sqrt(jnp.sqrt(jnp.sqrt(jnp.maximum(sums, 1e-36))))
    high = lax.reduce_precision(root, 5, 10)
    low = lax.reduce_precision((root - high) * 1024.0, 5, 10)
    return high.astype(jnp.float16), low.astype(jnp.float16), unpacked(high, low)


def unpacked(high, low):
    root = (high + low / 1024.0) / 16.0
    for _ in range(3):
        root = root * root
    return root


def on_square_grid(left_docs, right_docs):
    side = lax.axis_size("col")
    feat_total = left_docs.shape[1] * side
    rows, width = left_docs.shape[0], right_docs.shape[0]
    row, col = lax.axis_index("row"), lax.axis_index("col")
    at_home = (row >> 1) == (col >> 1)
    same = (row & 1) == (col & 1)

    def other_core(block):
        return moved(block, side, lambda r, c: (r ^ 1, c))

    nears, crosses = [], []
    first, second = lax.optimization_barrier((right_docs[:width // 2], right_docs[width // 2:]))
    for half in (first, second):
        if nears:
            half, _ = lax.optimization_barrier((half, nears[0]))
        swapped = moved(half, side, lambda r, c: (r ^ 2, c))
        near, leaving = lax.optimization_barrier((jnp.where(at_home, half, swapped), jnp.where(at_home, swapped, half)))
        nears.append(near)
        crosses.append(moved(leaving, side, lambda r, c: (r, c ^ 2)))
    left_other = moved(left_docs, side, lambda r, c: (r, c ^ 1))
    near = lax.optimization_barrier(jnp.concatenate(nears))
    near_other = other_core(near)
    crosses[1], near_other = lax.optimization_barrier((crosses[1], near_other))
    cross = lax.optimization_barrier(jnp.concatenate(crosses))
    lefts = lax.optimization_barrier((jnp.where(same, left_docs, left_other), jnp.where(same, left_other, left_docs)))

    def half_sum(mine, other):
        gram = sum(contract(left, right) for left, right in zip(lefts, (mine, other)))
        return gram, squares(mine) + squares(other)

    cross_gram = contract(lefts[0], cross)
    cross_other, cross_gram = lax.optimization_barrier((jnp.concatenate([other_core(part) for part in crosses]), cross_gram))
    cross_gram = cross_gram + contract(lefts[1], cross_other)
    cross_sq = squares(cross) + squares(cross_other)
    left_sq = squares(left_docs) + squares(left_other)

    left_high, left_low, left_read = packed(left_sq)
    right_high, right_low, right_read = packed(cross_sq)
    tile = cross_gram * (top * lax.rsqrt(left_read))[:, None] * lax.rsqrt(right_read)[None, :]
    parts = rows // width
    sums = [left_high.reshape(parts, width), left_low.reshape(parts, width), right_high[None], right_low[None]]
    spare = jnp.zeros((-(2 * parts + 2) % 8, width), jnp.float16)
    message = jnp.concatenate([tile.astype(jnp.float16), *sums, spare])
    got = moved(message, side, lambda r, c: (r, c ^ 2))

    near_other, _ = lax.optimization_barrier((near_other, message))
    near_gram, near_sq = half_sum(near, near_other)
    near_gram, got = lax.optimization_barrier((near_gram, got))
    got = got.astype(jnp.float32)
    sums = jnp.split(got[rows:rows + 2 * parts + 2], (parts, 2 * parts, 2 * parts + 1))
    left_got, right_got = unpacked(*sums[:2]).reshape(rows), unpacked(*sums[2:]).reshape(width)
    far_gram = got[:rows] * (jnp.sqrt(left_got) / top)[:, None] * jnp.sqrt(right_got)[None, :]
    return finish(near_gram + far_gram, left_sq + left_got, near_sq + right_got, feat_total)


def on_any_grid(left_docs, right_docs):
    feat_total = left_docs.shape[1] * lax.axis_size("col")
    right_all = lax.all_gather(right_docs, "row", axis=1, tiled=True)
    held = lax.all_to_all(right_all, "col", split_axis=1, concat_axis=0, tiled=True)
    summed = lax.psum_scatter(contract(left_docs, held), "col", scatter_dimension=1, tiled=True)
    left_sq = lax.psum(squares(left_docs), "col")
    right_sq = lax.psum(squares(right_docs), "row")
    return finish(summed, left_sq, right_sq, feat_total)


def solution(mesh):
    square = mesh.shape["row"] == mesh.shape["col"] == 4
    in_specs = (P(("bucket", "row"), "col"), P(("bucket", "col"), "row"))
    out_specs = P(("bucket", "row"), "col")
    return jax.shard_map(
        on_square_grid if square else on_any_grid,
        mesh=mesh, in_specs=in_specs, out_specs=out_specs, check_vma=False,
    )
```

```python
import jax
import jax.numpy as jnp
from jax import lax
from jax.sharding import PartitionSpec as P

epsilon = 1e-06
top = 2.0**15


def contract(left_part, right_part):
    return lax.dot_general(
        left_part, right_part, (((1,), (1,)), ((), ())), preferred_element_type=jnp.float32
    )


def squares(block_part):
    widened = block_part.astype(jnp.float32)
    return jnp.sum(widened * widened, axis=1)


def moved(value, side, place):
    pairs = []
    for row in range(side):
        for col in range(side):
            target = place(row, col)
            if target is not None:
                pairs.append((row * side + col, target[0] * side + target[1]))
    return lax.ppermute(value, ("row", "col"), pairs)


def finish(summed, left_sq, right_sq, feat_total):
    left_scale = lax.rsqrt(left_sq / feat_total + epsilon)
    right_scale = lax.rsqrt(right_sq / feat_total + epsilon)
    return summed / feat_total * left_scale[:, None] * right_scale[None, :]


def packed(sums):
    root = 16.0 * jnp.sqrt(jnp.sqrt(jnp.sqrt(jnp.maximum(sums, 1e-36))))
    high = lax.reduce_precision(root, 5, 10)
    low = lax.reduce_precision((root - high) * 1024.0, 5, 10)
    return high.astype(jnp.float16), low.astype(jnp.float16), unpacked(high, low)


def unpacked(high, low):
    root = (high + low / 1024.0) / 16.0
    for _ in range(3):
        root = root * root
    return root


def on_square_grid(left_docs, right_docs):
    side = lax.axis_size("col")
    feat_total = left_docs.shape[1] * side
    rows, width = left_docs.shape[0], right_docs.shape[0]
    row, col = lax.axis_index("row"), lax.axis_index("col")
    at_home = (row >> 1) == (col >> 1)
    same = (row & 1) == (col & 1)

    def other_core(block):
        return moved(block, side, lambda r, c: (r ^ 1, c))

    nears, crosses = [], []
    for half in lax.optimization_barrier((right_docs[:width // 2], right_docs[width // 2:])):
        swapped = moved(half, side, lambda r, c: (r ^ 2, c))
        pieces = jnp.split(jnp.where(at_home, swapped, half), 2)
        near, *leaving = lax.optimization_barrier((jnp.where(at_home, half, swapped), *pieces))
        nears.append(near)
        crosses.append(jnp.concatenate([moved(piece, side, lambda r, c: (r, c ^ 2)) for piece in leaving]))
    left_other = moved(left_docs, side, lambda r, c: (r, c ^ 1))
    near = lax.optimization_barrier(jnp.concatenate(nears))
    near_other = other_core(near)
    crosses[1], near_other = lax.optimization_barrier((crosses[1], near_other))
    cross = lax.optimization_barrier(jnp.concatenate(crosses))
    lefts = lax.optimization_barrier((jnp.where(same, left_docs, left_other), jnp.where(same, left_other, left_docs)))

    def half_sum(mine, other):
        gram = sum(contract(left, right) for left, right in zip(lefts, (mine, other)))
        return gram, squares(mine) + squares(other)

    cross_gram = contract(lefts[0], cross)
    cross_other, cross_gram = lax.optimization_barrier((jnp.concatenate([other_core(part) for part in crosses]), cross_gram))
    cross_gram = cross_gram + contract(lefts[1], cross_other)
    cross_sq = squares(cross) + squares(cross_other)
    left_sq = squares(left_docs) + squares(left_other)

    left_high, left_low, left_read = packed(left_sq)
    right_high, right_low, right_read = packed(cross_sq)
    tile = cross_gram * (top * lax.rsqrt(left_read))[:, None] * lax.rsqrt(right_read)[None, :]
    parts = rows // width
    sums = [left_high.reshape(parts, width), left_low.reshape(parts, width), right_high[None], right_low[None]]
    spare = jnp.zeros((-(2 * parts + 2) % 8, width), jnp.float16)
    message = jnp.concatenate([tile.astype(jnp.float16), *sums, spare])
    got = moved(message, side, lambda r, c: (r, c ^ 2))

    near_other, _ = lax.optimization_barrier((near_other, message))
    near_gram, near_sq = half_sum(near, near_other)
    near_gram, got = lax.optimization_barrier((near_gram, got))
    got = got.astype(jnp.float32)
    sums = jnp.split(got[rows:rows + 2 * parts + 2], (parts, 2 * parts, 2 * parts + 1))
    left_got, right_got = unpacked(*sums[:2]).reshape(rows), unpacked(*sums[2:]).reshape(width)
    far_gram = got[:rows] * (jnp.sqrt(left_got) / top)[:, None] * jnp.sqrt(right_got)[None, :]
    return finish(near_gram + far_gram, left_sq + left_got, near_sq + right_got, feat_total)


def on_any_grid(left_docs, right_docs):
    feat_total = left_docs.shape[1] * lax.axis_size("col")
    right_all = lax.all_gather(right_docs, "row", axis=1, tiled=True)
    held = lax.all_to_all(right_all, "col", split_axis=1, concat_axis=0, tiled=True)
    summed = lax.psum_scatter(contract(left_docs, held), "col", scatter_dimension=1, tiled=True)
    left_sq = lax.psum(squares(left_docs), "col")
    right_sq = lax.psum(squares(right_docs), "row")
    return finish(summed, left_sq, right_sq, feat_total)


def solution(mesh):
    square = mesh.shape["row"] == mesh.shape["col"] == 4
    in_specs = (P(("bucket", "row"), "col"), P(("bucket", "col"), "row"))
    out_specs = P(("bucket", "row"), "col")
    return jax.shard_map(
        on_square_grid if square else on_any_grid,
        mesh=mesh, in_specs=in_specs, out_specs=out_specs, check_vma=False,
    )
```

```python
import jax
import jax.numpy as jnp
from jax import lax
from jax.sharding import PartitionSpec as P

epsilon = 1e-06
top = 2.0**15


def contract(left_part, right_part):
    return lax.dot_general(
        left_part, right_part, (((1,), (1,)), ((), ())), preferred_element_type=jnp.float32
    )


def squares(block_part):
    widened = block_part.astype(jnp.float32)
    return jnp.sum(widened * widened, axis=1)


def moved(value, side, place):
    pairs = []
    for row in range(side):
        for col in range(side):
            target = place(row, col)
            if target is not None:
                pairs.append((row * side + col, target[0] * side + target[1]))
    return lax.ppermute(value, ("row", "col"), pairs)


def finish(summed, left_sq, right_sq, feat_total):
    left_scale = lax.rsqrt(left_sq / feat_total + epsilon)
    right_scale = lax.rsqrt(right_sq / feat_total + epsilon)
    return summed / feat_total * left_scale[:, None] * right_scale[None, :]


def packed(sums):
    root = 16.0 * jnp.sqrt(jnp.sqrt(jnp.sqrt(jnp.maximum(sums, 1e-36))))
    high = lax.reduce_precision(root, 5, 10)
    low = lax.reduce_precision((root - high) * 1024.0, 5, 10)
    return high.astype(jnp.float16), low.astype(jnp.float16), unpacked(high, low)


def unpacked(high, low):
    root = (high + low / 1024.0) / 16.0
    for _ in range(3):
        root = root * root
    return root


def on_square_grid(left_docs, right_docs):
    side = lax.axis_size("col")
    feat_total = left_docs.shape[1] * side
    rows, width = left_docs.shape[0], right_docs.shape[0]
    row, col = lax.axis_index("row"), lax.axis_index("col")
    at_home = (row >> 1) == (col >> 1)
    same = (row & 1) == (col & 1)

    def other_core(block):
        return moved(block, side, lambda r, c: (r ^ 1, c))

    nears, crosses = [], []
    for half in lax.optimization_barrier((right_docs[:width // 2], right_docs[width // 2:])):
        swapped = moved(half, side, lambda r, c: (r ^ 2, c))
        near, leaving = lax.optimization_barrier((jnp.where(at_home, half, swapped), jnp.where(at_home, swapped, half)))
        nears.append(near)
        crosses.append(moved(leaving, side, lambda r, c: (r, c ^ 2)))
    left_other = moved(left_docs, side, lambda r, c: (r, c ^ 1))
    near = lax.optimization_barrier(jnp.concatenate(nears))
    crosses[1], left_other = lax.optimization_barrier((crosses[1], left_other))
    cross = lax.optimization_barrier(jnp.concatenate(crosses))
    lefts = lax.optimization_barrier((jnp.where(same, left_docs, left_other), jnp.where(same, left_other, left_docs)))

    def half_sum(mine, other):
        gram = sum(contract(left, right) for left, right in zip(lefts, (mine, other)))
        return gram, squares(mine) + squares(other)

    near_other = other_core(near)
    cross_gram = contract(lefts[0], cross)
    cross_other, cross_gram = lax.optimization_barrier((jnp.concatenate([other_core(part) for part in crosses]), cross_gram))
    cross_gram = cross_gram + contract(lefts[1], cross_other)
    cross_sq = squares(cross) + squares(cross_other)
    left_sq = squares(left_docs) + squares(left_other)

    left_high, left_low, left_read = packed(left_sq)
    right_high, right_low, right_read = packed(cross_sq)
    tile = cross_gram * (top * lax.rsqrt(left_read))[:, None] * lax.rsqrt(right_read)[None, :]
    parts = rows // width
    sums = [left_high.reshape(parts, width), left_low.reshape(parts, width), right_high[None], right_low[None]]
    spare = jnp.zeros((-(2 * parts + 2) % 8, width), jnp.float16)
    message = jnp.concatenate([tile.astype(jnp.float16), *sums, spare])
    got = moved(message, side, lambda r, c: (r, c ^ 2))

    near, near_other, _ = lax.optimization_barrier((near, near_other, message))
    near_gram, near_sq = half_sum(near, near_other)
    near_gram, got = lax.optimization_barrier((near_gram, got))
    got = got.astype(jnp.float32)
    sums = jnp.split(got[rows:rows + 2 * parts + 2], (parts, 2 * parts, 2 * parts + 1))
    left_got, right_got = unpacked(*sums[:2]).reshape(rows), unpacked(*sums[2:]).reshape(width)
    far_gram = got[:rows] * (jnp.sqrt(left_got) / top)[:, None] * jnp.sqrt(right_got)[None, :]
    return finish(near_gram + far_gram, left_sq + left_got, near_sq + right_got, feat_total)


def on_any_grid(left_docs, right_docs):
    feat_total = left_docs.shape[1] * lax.axis_size("col")
    right_all = lax.all_gather(right_docs, "row", axis=1, tiled=True)
    held = lax.all_to_all(right_all, "col", split_axis=1, concat_axis=0, tiled=True)
    summed = lax.psum_scatter(contract(left_docs, held), "col", scatter_dimension=1, tiled=True)
    left_sq = lax.psum(squares(left_docs), "col")
    right_sq = lax.psum(squares(right_docs), "row")
    return finish(summed, left_sq, right_sq, feat_total)


def solution(mesh):
    square = mesh.shape["row"] == mesh.shape["col"] == 4
    in_specs = (P(("bucket", "row"), "col"), P(("bucket", "col"), "row"))
    out_specs = P(("bucket", "row"), "col")
    return jax.shard_map(
        on_square_grid if square else on_any_grid,
        mesh=mesh, in_specs=in_specs, out_specs=out_specs, check_vma=False,
    )
```

```python
import jax
import jax.numpy as jnp
from jax import lax
from jax.experimental import pallas as pl
from jax.experimental.pallas import tpu as pltpu
from jax.sharding import PartitionSpec as P

epsilon = 1e-06
top = 2.0**15


def contract(left_part, right_part):
    return lax.dot_general(
        left_part, right_part, (((1,), (1,)), ((), ())), preferred_element_type=jnp.float32
    )


def squares(block_part):
    widened = block_part.astype(jnp.float32)
    return jnp.sum(widened * widened, axis=1)


def moved(value, side, place):
    pairs = []
    for row in range(side):
        for col in range(side):
            target = place(row, col)
            if target is not None:
                pairs.append((row * side + col, target[0] * side + target[1]))
    return lax.ppermute(value, ("row", "col"), pairs)


def finish(summed, left_sq, right_sq, feat_total):
    left_scale = lax.rsqrt(left_sq / feat_total + epsilon)
    right_scale = lax.rsqrt(right_sq / feat_total + epsilon)
    return summed / feat_total * left_scale[:, None] * right_scale[None, :]


def packed(sums):
    root = 16.0 * jnp.sqrt(jnp.sqrt(jnp.sqrt(jnp.maximum(sums, 1e-36))))
    high = lax.reduce_precision(root, 5, 10)
    low = lax.reduce_precision((root - high) * 1024.0, 5, 10)
    return high.astype(jnp.float16), low.astype(jnp.float16), unpacked(high, low)


def unpacked(high, low):
    root = (high + low / 1024.0) / 16.0
    for _ in range(3):
        root = root * root
    return root


def parts_kernel(block, first, second, sems):
    cut = first.shape[0]
    copies = [
        pltpu.make_async_copy(block.at[pl.ds(0, cut)], first, sems.at[0]),
        pltpu.make_async_copy(block.at[pl.ds(cut, second.shape[0])], second, sems.at[1]),
    ]
    for copy in copies:
        copy.start()
    for copy in copies:
        copy.wait()


def parts_of(block, cut):
    rows, depth = block.shape
    return pl.pallas_call(
        parts_kernel,
        out_shape=[jax.ShapeDtypeStruct((part, depth), block.dtype) for part in (cut, rows - cut)],
        in_specs=[pl.BlockSpec(memory_space=pl.ANY)],
        out_specs=[pl.BlockSpec(memory_space=pltpu.VMEM)] * 2,
        scratch_shapes=[pltpu.SemaphoreType.DMA((2,))],
    )(block)


def on_square_grid(left_docs, right_docs):
    side = lax.axis_size("col")
    feat_total = left_docs.shape[1] * side
    rows, width = left_docs.shape[0], right_docs.shape[0]
    row, col = lax.axis_index("row"), lax.axis_index("col")
    at_home = (row >> 1) == (col >> 1)
    same = (row & 1) == (col & 1)

    def other_core(block):
        return moved(block, side, lambda r, c: (r ^ 1, c))

    nears, crosses = [], []
    for part in parts_of(right_docs, width // 2):
        swapped = moved(part, side, lambda r, c: (r ^ 2, c))
        near, leaving = lax.optimization_barrier((jnp.where(at_home, part, swapped), jnp.where(at_home, swapped, part)))
        nears.append(near)
        crosses.append(moved(leaving, side, lambda r, c: (r, c ^ 2)))
    left_other = moved(left_docs, side, lambda r, c: (r, c ^ 1))
    near = lax.optimization_barrier(jnp.concatenate(nears))
    near_other = other_core(near)
    crosses[1], near_other = lax.optimization_barrier((crosses[1], near_other))
    cross = lax.optimization_barrier(jnp.concatenate(crosses))
    lefts = lax.optimization_barrier((jnp.where(same, left_docs, left_other), jnp.where(same, left_other, left_docs)))

    def half_sum(mine, other):
        gram = sum(contract(left, right) for left, right in zip(lefts, (mine, other)))
        return gram, squares(mine) + squares(other)

    cross_gram = contract(lefts[0], cross)
    cross_other, cross_gram = lax.optimization_barrier((jnp.concatenate([other_core(part) for part in crosses]), cross_gram))
    cross_gram = cross_gram + contract(lefts[1], cross_other)
    cross_sq = squares(cross) + squares(cross_other)
    left_sq = squares(left_docs) + squares(left_other)

    left_high, left_low, left_read = packed(left_sq)
    right_high, right_low, right_read = packed(cross_sq)
    tile = cross_gram * (top * lax.rsqrt(left_read))[:, None] * lax.rsqrt(right_read)[None, :]
    parts = rows // width
    sums = [left_high.reshape(parts, width), left_low.reshape(parts, width), right_high[None], right_low[None]]
    spare = jnp.zeros((-(2 * parts + 2) % 8, width), jnp.float16)
    message = jnp.concatenate([tile.astype(jnp.float16), *sums, spare])
    got = moved(message, side, lambda r, c: (r, c ^ 2))

    near_other, _ = lax.optimization_barrier((near_other, message))
    near_gram, near_sq = half_sum(near, near_other)
    near_gram, got = lax.optimization_barrier((near_gram, got))
    got = got.astype(jnp.float32)
    sums = jnp.split(got[rows:rows + 2 * parts + 2], (parts, 2 * parts, 2 * parts + 1))
    left_got, right_got = unpacked(*sums[:2]).reshape(rows), unpacked(*sums[2:]).reshape(width)
    far_gram = got[:rows] * (jnp.sqrt(left_got) / top)[:, None] * jnp.sqrt(right_got)[None, :]
    return finish(near_gram + far_gram, left_sq + left_got, near_sq + right_got, feat_total)


def on_any_grid(left_docs, right_docs):
    feat_total = left_docs.shape[1] * lax.axis_size("col")
    right_all = lax.all_gather(right_docs, "row", axis=1, tiled=True)
    held = lax.all_to_all(right_all, "col", split_axis=1, concat_axis=0, tiled=True)
    summed = lax.psum_scatter(contract(left_docs, held), "col", scatter_dimension=1, tiled=True)
    left_sq = lax.psum(squares(left_docs), "col")
    right_sq = lax.psum(squares(right_docs), "row")
    return finish(summed, left_sq, right_sq, feat_total)


def solution(mesh):
    square = mesh.shape["row"] == mesh.shape["col"] == 4
    in_specs = (P(("bucket", "row"), "col"), P(("bucket", "col"), "row"))
    out_specs = P(("bucket", "row"), "col")
    return jax.shard_map(
        on_square_grid if square else on_any_grid,
        mesh=mesh, in_specs=in_specs, out_specs=out_specs, check_vma=False,
    )
```

```python
import jax
import jax.numpy as jnp
from jax import lax
from jax.sharding import PartitionSpec as P

epsilon = 1e-06
top = 2.0**15


def contract(left_part, right_part):
    return lax.dot_general(
        left_part, right_part, (((1,), (1,)), ((), ())), preferred_element_type=jnp.float32
    )


def squares(block_part):
    widened = block_part.astype(jnp.float32)
    return jnp.sum(widened * widened, axis=1)


def moved(value, side, place):
    pairs = []
    for row in range(side):
        for col in range(side):
            target = place(row, col)
            if target is not None:
                pairs.append((row * side + col, target[0] * side + target[1]))
    return lax.ppermute(value, ("row", "col"), pairs)


def finish(summed, left_sq, right_sq, feat_total):
    left_scale = lax.rsqrt(left_sq / feat_total + epsilon)
    right_scale = lax.rsqrt(right_sq / feat_total + epsilon)
    return summed / feat_total * left_scale[:, None] * right_scale[None, :]


def packed(sums):
    root = 16.0 * jnp.sqrt(jnp.sqrt(jnp.sqrt(jnp.maximum(sums, 1e-36))))
    high = lax.reduce_precision(root, 5, 10)
    low = lax.reduce_precision((root - high) * 1024.0, 5, 10)
    return high.astype(jnp.float16), low.astype(jnp.float16), unpacked(high, low)


def unpacked(high, low):
    root = (high + low / 1024.0) / 16.0
    for _ in range(3):
        root = root * root
    return root


def on_square_grid(left_docs, right_docs):
    side = lax.axis_size("col")
    feat_total = left_docs.shape[1] * side
    rows, width = left_docs.shape[0], right_docs.shape[0]
    row, col = lax.axis_index("row"), lax.axis_index("col")
    at_home = (row >> 1) == (col >> 1)
    same = (row & 1) == (col & 1)

    def other_core(block):
        return moved(block, side, lambda r, c: (r ^ 1, c))

    nears, crosses = [], []
    for half in lax.optimization_barrier((right_docs[:width // 2], right_docs[width // 2:])):
        swapped = moved(half, side, lambda r, c: (r ^ 2, c))
        near, leaving = lax.optimization_barrier((jnp.where(at_home, half, swapped), jnp.where(at_home, swapped, half)))
        nears.append(near)
        crosses.append(moved(leaving, side, lambda r, c: (r, c ^ 2)))
    left_other = moved(left_docs, side, lambda r, c: (r, c ^ 1))
    near = lax.optimization_barrier(jnp.concatenate(nears))
    near_other = other_core(near)
    crosses[1], near_other = lax.optimization_barrier((crosses[1], near_other))
    cross = lax.optimization_barrier(jnp.concatenate(crosses))
    lefts = lax.optimization_barrier((jnp.where(same, left_docs, left_other), jnp.where(same, left_other, left_docs)))

    def half_sum(mine, other):
        gram = sum(contract(left, right) for left, right in zip(lefts, (mine, other)))
        return gram, squares(mine) + squares(other)

    cross_gram = contract(lefts[0], cross)
    cross_other, _ = lax.optimization_barrier((jnp.concatenate([other_core(part) for part in crosses]), cross_gram))
    cross_gram = cross_gram + contract(lefts[1], cross_other)
    cross_sq = squares(cross) + squares(cross_other)
    left_sq = squares(left_docs) + squares(left_other)

    left_high, left_low, left_read = packed(left_sq)
    right_high, right_low, right_read = packed(cross_sq)
    tile = cross_gram * (top * lax.rsqrt(left_read))[:, None] * lax.rsqrt(right_read)[None, :]
    parts = rows // width
    sums = [left_high.reshape(parts, width), left_low.reshape(parts, width), right_high[None], right_low[None]]
    spare = jnp.zeros((-(2 * parts + 2) % 8, width), jnp.float16)
    message = jnp.concatenate([tile.astype(jnp.float16), *sums, spare])
    got = moved(message, side, lambda r, c: (r, c ^ 2))

    near_other, _ = lax.optimization_barrier((near_other, message))
    near_gram, near_sq = half_sum(near, near_other)
    near_gram, got = lax.optimization_barrier((near_gram, got))
    got = got.astype(jnp.float32)
    sums = jnp.split(got[rows:rows + 2 * parts + 2], (parts, 2 * parts, 2 * parts + 1))
    left_got, right_got = unpacked(*sums[:2]).reshape(rows), unpacked(*sums[2:]).reshape(width)
    far_gram = got[:rows] * (jnp.sqrt(left_got) / top)[:, None] * jnp.sqrt(right_got)[None, :]
    return finish(near_gram + far_gram, left_sq + left_got, near_sq + right_got, feat_total)


def on_any_grid(left_docs, right_docs):
    feat_total = left_docs.shape[1] * lax.axis_size("col")
    right_all = lax.all_gather(right_docs, "row", axis=1, tiled=True)
    held = lax.all_to_all(right_all, "col", split_axis=1, concat_axis=0, tiled=True)
    summed = lax.psum_scatter(contract(left_docs, held), "col", scatter_dimension=1, tiled=True)
    left_sq = lax.psum(squares(left_docs), "col")
    right_sq = lax.psum(squares(right_docs), "row")
    return finish(summed, left_sq, right_sq, feat_total)


def solution(mesh):
    square = mesh.shape["row"] == mesh.shape["col"] == 4
    in_specs = (P(("bucket", "row"), "col"), P(("bucket", "col"), "row"))
    out_specs = P(("bucket", "row"), "col")
    return jax.shard_map(
        on_square_grid if square else on_any_grid,
        mesh=mesh, in_specs=in_specs, out_specs=out_specs, check_vma=False,
    )
```

```python
import jax
import jax.numpy as jnp
from jax import lax
from jax.sharding import PartitionSpec as P

epsilon = 1e-06
top = 2.0**15


def contract(left_part, right_part):
    return lax.dot_general(
        left_part, right_part, (((1,), (1,)), ((), ())), preferred_element_type=jnp.float32
    )


def squares(block_part):
    widened = block_part.astype(jnp.float32)
    return jnp.sum(widened * widened, axis=1)


def moved(value, side, place):
    pairs = []
    for row in range(side):
        for col in range(side):
            target = place(row, col)
            if target is not None:
                pairs.append((row * side + col, target[0] * side + target[1]))
    return lax.ppermute(value, ("row", "col"), pairs)


def finish(summed, left_sq, right_sq, feat_total):
    left_scale = lax.rsqrt(left_sq / feat_total + epsilon)
    right_scale = lax.rsqrt(right_sq / feat_total + epsilon)
    return summed / feat_total * left_scale[:, None] * right_scale[None, :]


def packed(sums):
    root = 16.0 * jnp.sqrt(jnp.sqrt(jnp.sqrt(jnp.maximum(sums, 1e-36))))
    high = lax.reduce_precision(root, 5, 10)
    low = lax.reduce_precision((root - high) * 1024.0, 5, 10)
    return high.astype(jnp.float16), low.astype(jnp.float16), unpacked(high, low)


def unpacked(high, low):
    root = (high + low / 1024.0) / 16.0
    for _ in range(3):
        root = root * root
    return root


def on_square_grid(left_docs, right_docs):
    side = lax.axis_size("col")
    feat_total = left_docs.shape[1] * side
    rows, width = left_docs.shape[0], right_docs.shape[0]
    row, col = lax.axis_index("row"), lax.axis_index("col")
    at_home = (row >> 1) == (col >> 1)
    same = (row & 1) == (col & 1)

    def other_core(block):
        return moved(block, side, lambda r, c: (r ^ 1, c))

    nears, crosses = [], []
    for half in lax.optimization_barrier((right_docs[:width // 2], right_docs[width // 2:])):
        swapped = moved(half, side, lambda r, c: (r ^ 2, c))
        near, leaving = lax.optimization_barrier((jnp.where(at_home, half, swapped), jnp.where(at_home, swapped, half)))
        nears.append(near)
        crosses.append(moved(leaving, side, lambda r, c: (r, c ^ 2)))
    left_other = moved(left_docs, side, lambda r, c: (r, c ^ 1))
    near = lax.optimization_barrier(jnp.concatenate(nears))
    near_other = other_core(near)
    crosses[1], near_other = lax.optimization_barrier((crosses[1], near_other))
    cross = lax.optimization_barrier(jnp.concatenate(crosses))
    lefts = lax.optimization_barrier((jnp.where(same, left_docs, left_other), jnp.where(same, left_other, left_docs)))

    def half_sum(mine, other):
        gram = sum(contract(left, right) for left, right in zip(lefts, (mine, other)))
        return gram, squares(mine) + squares(other)

    cross_gram = contract(lefts[0], cross)
    others = [other_core(part) for part in crosses]
    others[1], _ = lax.optimization_barrier((others[1], cross_gram))
    cross_other = lax.optimization_barrier(jnp.concatenate(others))
    cross_gram = cross_gram + contract(lefts[1], cross_other)
    cross_sq = squares(cross) + jnp.concatenate([squares(part) for part in others])
    left_sq = squares(left_docs) + squares(left_other)

    left_high, left_low, left_read = packed(left_sq)
    right_high, right_low, right_read = packed(cross_sq)
    tile = cross_gram * (top * lax.rsqrt(left_read))[:, None] * lax.rsqrt(right_read)[None, :]
    parts = rows // width
    sums = [left_high.reshape(parts, width), left_low.reshape(parts, width), right_high[None], right_low[None]]
    spare = jnp.zeros((-(2 * parts + 2) % 8, width), jnp.float16)
    message = jnp.concatenate([tile.astype(jnp.float16), *sums, spare])
    got = moved(message, side, lambda r, c: (r, c ^ 2))

    near_other, _ = lax.optimization_barrier((near_other, message))
    near_gram, near_sq = half_sum(near, near_other)
    near_gram, got = lax.optimization_barrier((near_gram, got))
    got = got.astype(jnp.float32)
    sums = jnp.split(got[rows:rows + 2 * parts + 2], (parts, 2 * parts, 2 * parts + 1))
    left_got, right_got = unpacked(*sums[:2]).reshape(rows), unpacked(*sums[2:]).reshape(width)
    far_gram = got[:rows] * (jnp.sqrt(left_got) / top)[:, None] * jnp.sqrt(right_got)[None, :]
    return finish(near_gram + far_gram, left_sq + left_got, near_sq + right_got, feat_total)


def on_any_grid(left_docs, right_docs):
    feat_total = left_docs.shape[1] * lax.axis_size("col")
    right_all = lax.all_gather(right_docs, "row", axis=1, tiled=True)
    held = lax.all_to_all(right_all, "col", split_axis=1, concat_axis=0, tiled=True)
    summed = lax.psum_scatter(contract(left_docs, held), "col", scatter_dimension=1, tiled=True)
    left_sq = lax.psum(squares(left_docs), "col")
    right_sq = lax.psum(squares(right_docs), "row")
    return finish(summed, left_sq, right_sq, feat_total)


def solution(mesh):
    square = mesh.shape["row"] == mesh.shape["col"] == 4
    in_specs = (P(("bucket", "row"), "col"), P(("bucket", "col"), "row"))
    out_specs = P(("bucket", "row"), "col")
    return jax.shard_map(
        on_square_grid if square else on_any_grid,
        mesh=mesh, in_specs=in_specs, out_specs=out_specs, check_vma=False,
    )
```

```python
import jax
import jax.numpy as jnp
from jax import lax
from jax.sharding import PartitionSpec as P

epsilon = 1e-06
top = 2.0**15


def contract(left_part, right_part):
    return lax.dot_general(
        left_part, right_part, (((1,), (1,)), ((), ())), preferred_element_type=jnp.float32
    )


def squares(block_part):
    widened = block_part.astype(jnp.float32)
    return jnp.sum(widened * widened, axis=1)


def moved(value, side, place):
    pairs = []
    for row in range(side):
        for col in range(side):
            target = place(row, col)
            if target is not None:
                pairs.append((row * side + col, target[0] * side + target[1]))
    return lax.ppermute(value, ("row", "col"), pairs)


def finish(summed, left_sq, right_sq, feat_total):
    left_scale = lax.rsqrt(left_sq / feat_total + epsilon)
    right_scale = lax.rsqrt(right_sq / feat_total + epsilon)
    return summed / feat_total * left_scale[:, None] * right_scale[None, :]


def packed(sums):
    root = 16.0 * jnp.sqrt(jnp.sqrt(jnp.sqrt(jnp.maximum(sums, 1e-36))))
    high = lax.reduce_precision(root, 5, 10)
    low = lax.reduce_precision((root - high) * 1024.0, 5, 10)
    return high.astype(jnp.float16), low.astype(jnp.float16), unpacked(high, low)


def unpacked(high, low):
    root = (high + low / 1024.0) / 16.0
    for _ in range(3):
        root = root * root
    return root


def on_square_grid(left_docs, right_docs):
    side = lax.axis_size("col")
    feat_total = left_docs.shape[1] * side
    rows, width = left_docs.shape[0], right_docs.shape[0]
    row, col = lax.axis_index("row"), lax.axis_index("col")
    at_home = (row >> 1) == (col >> 1)
    same = (row & 1) == (col & 1)

    def other_core(block):
        return moved(block, side, lambda r, c: (r ^ 1, c))

    nears, crosses = [], []
    for half in lax.optimization_barrier((right_docs[:width // 2], right_docs[width // 2:])):
        swapped = moved(half, side, lambda r, c: (r ^ 2, c))
        near, leaving = lax.optimization_barrier((jnp.where(at_home, half, swapped), jnp.where(at_home, swapped, half)))
        nears.append(near)
        crosses.append(moved(leaving, side, lambda r, c: (r, c ^ 2)))
    left_other = moved(left_docs, side, lambda r, c: (r, c ^ 1))
    near = lax.optimization_barrier(jnp.concatenate(nears))
    near_other = other_core(near)
    crosses[1], near_other = lax.optimization_barrier((crosses[1], near_other))
    cross = lax.optimization_barrier(jnp.concatenate(crosses))
    lefts = lax.optimization_barrier((jnp.where(same, left_docs, left_other), jnp.where(same, left_other, left_docs)))

    def half_sum(mine, other):
        gram = sum(contract(left, right) for left, right in zip(lefts, (mine, other)))
        return gram, squares(mine) + squares(other)

    cross_gram = contract(lefts[0], cross)
    cross_other, _ = lax.optimization_barrier((other_core(cross), cross_gram))
    cross_gram = cross_gram + contract(lefts[1], cross_other)
    cross_sq = squares(cross) + squares(cross_other)
    left_sq = squares(left_docs) + squares(left_other)

    left_high, left_low, left_read = packed(left_sq)
    right_high, right_low, right_read = packed(cross_sq)
    tile = cross_gram * (top * lax.rsqrt(left_read))[:, None] * lax.rsqrt(right_read)[None, :]
    parts = rows // width
    sums = [left_high.reshape(parts, width), left_low.reshape(parts, width), right_high[None], right_low[None]]
    spare = jnp.zeros((-(2 * parts + 2) % 8, width), jnp.float16)
    message = jnp.concatenate([tile.astype(jnp.float16), *sums, spare])
    got = moved(message, side, lambda r, c: (r, c ^ 2))

    near_other, _ = lax.optimization_barrier((near_other, message))
    near_gram, near_sq = half_sum(near, near_other)
    near_gram, got = lax.optimization_barrier((near_gram, got))
    got = got.astype(jnp.float32)
    sums = jnp.split(got[rows:rows + 2 * parts + 2], (parts, 2 * parts, 2 * parts + 1))
    left_got, right_got = unpacked(*sums[:2]).reshape(rows), unpacked(*sums[2:]).reshape(width)
    far_gram = got[:rows] * (jnp.sqrt(left_got) / top)[:, None] * jnp.sqrt(right_got)[None, :]
    return finish(near_gram + far_gram, left_sq + left_got, near_sq + right_got, feat_total)


def on_any_grid(left_docs, right_docs):
    feat_total = left_docs.shape[1] * lax.axis_size("col")
    right_all = lax.all_gather(right_docs, "row", axis=1, tiled=True)
    held = lax.all_to_all(right_all, "col", split_axis=1, concat_axis=0, tiled=True)
    summed = lax.psum_scatter(contract(left_docs, held), "col", scatter_dimension=1, tiled=True)
    left_sq = lax.psum(squares(left_docs), "col")
    right_sq = lax.psum(squares(right_docs), "row")
    return finish(summed, left_sq, right_sq, feat_total)


def solution(mesh):
    square = mesh.shape["row"] == mesh.shape["col"] == 4
    in_specs = (P(("bucket", "row"), "col"), P(("bucket", "col"), "row"))
    out_specs = P(("bucket", "row"), "col")
    return jax.shard_map(
        on_square_grid if square else on_any_grid,
        mesh=mesh, in_specs=in_specs, out_specs=out_specs, check_vma=False,
    )
```

```python
import jax
import jax.numpy as jnp
from jax import lax
from jax.sharding import PartitionSpec as P

epsilon = 1e-06
top = 2.0**15


def contract(left_part, right_part):
    return lax.dot_general(
        left_part, right_part, (((1,), (1,)), ((), ())), preferred_element_type=jnp.float32
    )


def squares(block_part):
    widened = block_part.astype(jnp.float32)
    return jnp.sum(widened * widened, axis=1)


def moved(value, side, place):
    pairs = []
    for row in range(side):
        for col in range(side):
            target = place(row, col)
            if target is not None:
                pairs.append((row * side + col, target[0] * side + target[1]))
    return lax.ppermute(value, ("row", "col"), pairs)


def finish(summed, left_sq, right_sq, feat_total):
    left_scale = lax.rsqrt(left_sq / feat_total + epsilon)
    right_scale = lax.rsqrt(right_sq / feat_total + epsilon)
    return summed / feat_total * left_scale[:, None] * right_scale[None, :]


def packed(sums):
    root = 16.0 * jnp.sqrt(jnp.sqrt(jnp.sqrt(jnp.maximum(sums, 1e-36))))
    high = lax.reduce_precision(root, 5, 10)
    low = lax.reduce_precision((root - high) * 1024.0, 5, 10)
    return high.astype(jnp.float16), low.astype(jnp.float16), unpacked(high, low)


def unpacked(high, low):
    root = (high + low / 1024.0) / 16.0
    for _ in range(3):
        root = root * root
    return root


def on_square_grid(left_docs, right_docs):
    side = lax.axis_size("col")
    feat_total = left_docs.shape[1] * side
    rows, width = left_docs.shape[0], right_docs.shape[0]
    row, col = lax.axis_index("row"), lax.axis_index("col")
    at_home = (row >> 1) == (col >> 1)
    same = (row & 1) == (col & 1)

    def other_core(block):
        return moved(block, side, lambda r, c: (r ^ 1, c))

    nears, crosses = [], []
    for half in lax.optimization_barrier((right_docs[:width // 2], right_docs[width // 2:])):
        swapped = moved(half, side, lambda r, c: (r ^ 2, c))
        near, leaving = lax.optimization_barrier((jnp.where(at_home, half, swapped), jnp.where(at_home, swapped, half)))
        nears.append(near)
        crosses.append(moved(leaving, side, lambda r, c: (r, c ^ 2)))
    left_other = moved(left_docs, side, lambda r, c: (r, c ^ 1))
    near = lax.optimization_barrier(jnp.concatenate(nears))
    near_other = other_core(near)
    crosses[1], near_other = lax.optimization_barrier((crosses[1], near_other))
    cross = lax.optimization_barrier(jnp.concatenate(crosses))
    lefts = lax.optimization_barrier((jnp.where(same, left_docs, left_other), jnp.where(same, left_other, left_docs)))

    def half_sum(mine, other):
        gram = sum(contract(left, right) for left, right in zip(lefts, (mine, other)))
        return gram, squares(mine) + squares(other)

    cross_gram = contract(lefts[0], cross)
    left_late, _ = lax.optimization_barrier((left_other, cross_gram))
    cross_other, _ = lax.optimization_barrier((jnp.concatenate([other_core(part) for part in crosses]), cross_gram))
    cross_gram = cross_gram + contract(lefts[1], cross_other)
    cross_sq = squares(cross) + squares(cross_other)
    left_sq = squares(left_docs) + squares(left_late)

    left_high, left_low, left_read = packed(left_sq)
    right_high, right_low, right_read = packed(cross_sq)
    tile = cross_gram * (top * lax.rsqrt(left_read))[:, None] * lax.rsqrt(right_read)[None, :]
    parts = rows // width
    sums = [left_high.reshape(parts, width), left_low.reshape(parts, width), right_high[None], right_low[None]]
    spare = jnp.zeros((-(2 * parts + 2) % 8, width), jnp.float16)
    message = jnp.concatenate([tile.astype(jnp.float16), *sums, spare])
    got = moved(message, side, lambda r, c: (r, c ^ 2))

    near_other, _ = lax.optimization_barrier((near_other, message))
    near_gram, near_sq = half_sum(near, near_other)
    near_gram, got = lax.optimization_barrier((near_gram, got))
    got = got.astype(jnp.float32)
    sums = jnp.split(got[rows:rows + 2 * parts + 2], (parts, 2 * parts, 2 * parts + 1))
    left_got, right_got = unpacked(*sums[:2]).reshape(rows), unpacked(*sums[2:]).reshape(width)
    far_gram = got[:rows] * (jnp.sqrt(left_got) / top)[:, None] * jnp.sqrt(right_got)[None, :]
    return finish(near_gram + far_gram, left_sq + left_got, near_sq + right_got, feat_total)


def on_any_grid(left_docs, right_docs):
    feat_total = left_docs.shape[1] * lax.axis_size("col")
    right_all = lax.all_gather(right_docs, "row", axis=1, tiled=True)
    held = lax.all_to_all(right_all, "col", split_axis=1, concat_axis=0, tiled=True)
    summed = lax.psum_scatter(contract(left_docs, held), "col", scatter_dimension=1, tiled=True)
    left_sq = lax.psum(squares(left_docs), "col")
    right_sq = lax.psum(squares(right_docs), "row")
    return finish(summed, left_sq, right_sq, feat_total)


def solution(mesh):
    square = mesh.shape["row"] == mesh.shape["col"] == 4
    in_specs = (P(("bucket", "row"), "col"), P(("bucket", "col"), "row"))
    out_specs = P(("bucket", "row"), "col")
    return jax.shard_map(
        on_square_grid if square else on_any_grid,
        mesh=mesh, in_specs=in_specs, out_specs=out_specs, check_vma=False,
    )
```

```python
import jax
import jax.numpy as jnp
from jax import lax
from jax.sharding import PartitionSpec as P

epsilon = 1e-06
top = 2.0**15


def contract(left_part, right_part):
    return lax.dot_general(
        left_part, right_part, (((1,), (1,)), ((), ())), preferred_element_type=jnp.float32
    )


def squares(block_part):
    widened = block_part.astype(jnp.float32)
    return jnp.sum(widened * widened, axis=1)


def moved(value, side, place):
    pairs = []
    for row in range(side):
        for col in range(side):
            target = place(row, col)
            if target is not None:
                pairs.append((row * side + col, target[0] * side + target[1]))
    return lax.ppermute(value, ("row", "col"), pairs)


def finish(summed, left_sq, right_sq, feat_total):
    left_scale = lax.rsqrt(left_sq / feat_total + epsilon)
    right_scale = lax.rsqrt(right_sq / feat_total + epsilon)
    return summed / feat_total * left_scale[:, None] * right_scale[None, :]


def packed(sums):
    root = 16.0 * jnp.sqrt(jnp.sqrt(jnp.sqrt(jnp.maximum(sums, 1e-36))))
    high = lax.reduce_precision(root, 5, 10)
    low = lax.reduce_precision((root - high) * 1024.0, 5, 10)
    return high.astype(jnp.float16), low.astype(jnp.float16), unpacked(high, low)


def unpacked(high, low):
    root = (high + low / 1024.0) / 16.0
    for _ in range(3):
        root = root * root
    return root


def on_square_grid(left_docs, right_docs):
    side = lax.axis_size("col")
    feat_total = left_docs.shape[1] * side
    rows, width = left_docs.shape[0], right_docs.shape[0]
    row, col = lax.axis_index("row"), lax.axis_index("col")
    at_home = (row >> 1) == (col >> 1)
    same = (row & 1) == (col & 1)

    def other_core(block):
        return moved(block, side, lambda r, c: (r ^ 1, c))

    nears, crosses = [], []
    for half in lax.optimization_barrier((right_docs[:width // 2], right_docs[width // 2:])):
        swapped = moved(half, side, lambda r, c: (r ^ 2, c))
        near, leaving = lax.optimization_barrier((jnp.where(at_home, half, swapped), jnp.where(at_home, swapped, half)))
        nears.append(near)
        crosses.append(moved(leaving, side, lambda r, c: (r, c ^ 2)))
    left_other = moved(left_docs, side, lambda r, c: (r, c ^ 1))
    near = lax.optimization_barrier(jnp.concatenate(nears))
    near_other = other_core(near)
    crosses[1], near_other, left_other = lax.optimization_barrier((crosses[1], near_other, left_other))
    cross = lax.optimization_barrier(jnp.concatenate(crosses))
    lefts = lax.optimization_barrier((jnp.where(same, left_docs, left_other), jnp.where(same, left_other, left_docs)))

    def half_sum(mine, other):
        gram = sum(contract(left, right) for left, right in zip(lefts, (mine, other)))
        return gram, squares(mine) + squares(other)

    cross_gram = contract(lefts[0], cross)
    cross_other, _ = lax.optimization_barrier((jnp.concatenate([other_core(part) for part in crosses]), cross_gram))
    cross_gram = cross_gram + contract(lefts[1], cross_other)
    cross_sq = squares(cross) + squares(cross_other)
    left_sq = squares(left_docs) + squares(left_other)

    left_high, left_low, left_read = packed(left_sq)
    right_high, right_low, right_read = packed(cross_sq)
    tile = cross_gram * (top * lax.rsqrt(left_read))[:, None] * lax.rsqrt(right_read)[None, :]
    parts = rows // width
    sums = [left_high.reshape(parts, width), left_low.reshape(parts, width), right_high[None], right_low[None]]
    spare = jnp.zeros((-(2 * parts + 2) % 8, width), jnp.float16)
    message = jnp.concatenate([tile.astype(jnp.float16), *sums, spare])
    got = moved(message, side, lambda r, c: (r, c ^ 2))

    near_other, _ = lax.optimization_barrier((near_other, message))
    near_gram, near_sq = half_sum(near, near_other)
    near_gram, got = lax.optimization_barrier((near_gram, got))
    got = got.astype(jnp.float32)
    sums = jnp.split(got[rows:rows + 2 * parts + 2], (parts, 2 * parts, 2 * parts + 1))
    left_got, right_got = unpacked(*sums[:2]).reshape(rows), unpacked(*sums[2:]).reshape(width)
    far_gram = got[:rows] * (jnp.sqrt(left_got) / top)[:, None] * jnp.sqrt(right_got)[None, :]
    return finish(near_gram + far_gram, left_sq + left_got, near_sq + right_got, feat_total)


def on_any_grid(left_docs, right_docs):
    feat_total = left_docs.shape[1] * lax.axis_size("col")
    right_all = lax.all_gather(right_docs, "row", axis=1, tiled=True)
    held = lax.all_to_all(right_all, "col", split_axis=1, concat_axis=0, tiled=True)
    summed = lax.psum_scatter(contract(left_docs, held), "col", scatter_dimension=1, tiled=True)
    left_sq = lax.psum(squares(left_docs), "col")
    right_sq = lax.psum(squares(right_docs), "row")
    return finish(summed, left_sq, right_sq, feat_total)


def solution(mesh):
    square = mesh.shape["row"] == mesh.shape["col"] == 4
    in_specs = (P(("bucket", "row"), "col"), P(("bucket", "col"), "row"))
    out_specs = P(("bucket", "row"), "col")
    return jax.shard_map(
        on_square_grid if square else on_any_grid,
        mesh=mesh, in_specs=in_specs, out_specs=out_specs, check_vma=False,
    )
```

```python
import jax
import jax.numpy as jnp
from jax import lax
from jax.sharding import PartitionSpec as P

epsilon = 1e-06
top = 2.0**15


def contract(left_part, right_part):
    return lax.dot_general(
        left_part, right_part, (((1,), (1,)), ((), ())), preferred_element_type=jnp.float32
    )


def squares(block_part):
    widened = block_part.astype(jnp.float32)
    return jnp.sum(widened * widened, axis=1)


def moved(value, side, place):
    pairs = []
    for row in range(side):
        for col in range(side):
            target = place(row, col)
            if target is not None:
                pairs.append((row * side + col, target[0] * side + target[1]))
    return lax.ppermute(value, ("row", "col"), pairs)


def finish(summed, left_sq, right_sq, feat_total):
    left_scale = lax.rsqrt(left_sq / feat_total + epsilon)
    right_scale = lax.rsqrt(right_sq / feat_total + epsilon)
    return summed / feat_total * left_scale[:, None] * right_scale[None, :]


def packed(sums):
    root = 16.0 * jnp.sqrt(jnp.sqrt(jnp.sqrt(jnp.maximum(sums, 1e-36))))
    high = lax.reduce_precision(root, 5, 10)
    low = lax.reduce_precision((root - high) * 1024.0, 5, 10)
    return high.astype(jnp.float16), low.astype(jnp.float16), unpacked(high, low)


def unpacked(high, low):
    root = (high + low / 1024.0) / 16.0
    for _ in range(3):
        root = root * root
    return root


def on_square_grid(left_docs, right_docs):
    side = lax.axis_size("col")
    feat_total = left_docs.shape[1] * side
    rows, width = left_docs.shape[0], right_docs.shape[0]
    row, col = lax.axis_index("row"), lax.axis_index("col")
    at_home = (row >> 1) == (col >> 1)
    same = (row & 1) == (col & 1)

    def other_core(block):
        return moved(block, side, lambda r, c: (r ^ 1, c))

    nears, crosses = [], []
    for half in lax.optimization_barrier((right_docs[:width // 2], right_docs[width // 2:])):
        swapped = moved(half, side, lambda r, c: (r ^ 2, c))
        near, leaving = lax.optimization_barrier((jnp.where(at_home, half, swapped), jnp.where(at_home, swapped, half)))
        nears.append(near)
        crosses.append(moved(leaving, side, lambda r, c: (r, c ^ 2)))
    left_other = moved(left_docs, side, lambda r, c: (r, c ^ 1))
    near = lax.optimization_barrier(jnp.concatenate(nears))
    near_other = other_core(near)
    crosses[1], near_other = lax.optimization_barrier((crosses[1], near_other))
    cross = lax.optimization_barrier(jnp.concatenate(crosses))
    lefts = lax.optimization_barrier((jnp.where(same, left_docs, left_other), jnp.where(same, left_other, left_docs)))

    def half_sum(mine, other):
        gram = sum(contract(left, right) for left, right in zip(lefts, (mine, other)))
        return gram, squares(mine) + squares(other)

    cross_gram = contract(lefts[0], cross)
    cross_other, _ = lax.optimization_barrier((jnp.concatenate([other_core(part) for part in crosses]), cross_gram))
    cross_gram = cross_gram + contract(lefts[1], cross_other)
    cross_sq = jnp.concatenate([squares(part) for part in crosses]) + squares(cross_other)
    left_sq = squares(left_docs) + squares(left_other)

    left_high, left_low, left_read = packed(left_sq)
    right_high, right_low, right_read = packed(cross_sq)
    tile = cross_gram * (top * lax.rsqrt(left_read))[:, None] * lax.rsqrt(right_read)[None, :]
    parts = rows // width
    sums = [left_high.reshape(parts, width), left_low.reshape(parts, width), right_high[None], right_low[None]]
    spare = jnp.zeros((-(2 * parts + 2) % 8, width), jnp.float16)
    message = jnp.concatenate([tile.astype(jnp.float16), *sums, spare])
    got = moved(message, side, lambda r, c: (r, c ^ 2))

    near_other, _ = lax.optimization_barrier((near_other, message))
    near_gram, near_sq = half_sum(near, near_other)
    near_gram, got = lax.optimization_barrier((near_gram, got))
    got = got.astype(jnp.float32)
    sums = jnp.split(got[rows:rows + 2 * parts + 2], (parts, 2 * parts, 2 * parts + 1))
    left_got, right_got = unpacked(*sums[:2]).reshape(rows), unpacked(*sums[2:]).reshape(width)
    far_gram = got[:rows] * (jnp.sqrt(left_got) / top)[:, None] * jnp.sqrt(right_got)[None, :]
    return finish(near_gram + far_gram, left_sq + left_got, near_sq + right_got, feat_total)


def on_any_grid(left_docs, right_docs):
    feat_total = left_docs.shape[1] * lax.axis_size("col")
    right_all = lax.all_gather(right_docs, "row", axis=1, tiled=True)
    held = lax.all_to_all(right_all, "col", split_axis=1, concat_axis=0, tiled=True)
    summed = lax.psum_scatter(contract(left_docs, held), "col", scatter_dimension=1, tiled=True)
    left_sq = lax.psum(squares(left_docs), "col")
    right_sq = lax.psum(squares(right_docs), "row")
    return finish(summed, left_sq, right_sq, feat_total)


def solution(mesh):
    square = mesh.shape["row"] == mesh.shape["col"] == 4
    in_specs = (P(("bucket", "row"), "col"), P(("bucket", "col"), "row"))
    out_specs = P(("bucket", "row"), "col")
    return jax.shard_map(
        on_square_grid if square else on_any_grid,
        mesh=mesh, in_specs=in_specs, out_specs=out_specs, check_vma=False,
    )
```
